512 devices in a mesh: blk: 128 (over z, y, core), uly: 4 (over x).
Axes of the slice: x: 4, y: 4, z: 16, core: 2. Of those that a mesh axis runs over, the one named last changes fastest.
Arguments:
- queries: bfloat16 [65536, 2048], P(('blk', 'uly')), may hold values from -10 to 10
- keys: bfloat16 [65536, 512], P(('blk', 'uly')), may hold values from -8 to 8
- values: bfloat16 [65536, 512], P(('blk', 'uly')), may hold values from -6 to 6
- out_grad: bfloat16 [65536, 2048], P(('blk', 'uly')), may hold values from -6 to 6
- docs: int32 [65536], P(('blk', 'uly')), may hold values from 0 to 126, never falling along the last dimension, each value on 1 to 1025 neighbouring positions
Outputs:
- attended: bfloat16 [65536, 2048], P(('blk', 'uly'))
- query_grad: float32 [65536, 2048], P(('blk', 'uly'))
- key_grad: float32 [65536, 512], P(('blk', 'uly'))
- value_grad: float32 [65536, 512], P(('blk', 'uly'))
The draws below stay inside these ranges and needn't reach their ends.
Inputs may be any that keep to these rules, and one draw needn't show every extreme that they name: `docs`: document ids never fall along the sequence; each document holds 1 to 1025 consecutive tokens, and one holds exactly 1025.
All inputs are finite; a program needn't handle non-finite values.
Results may differ from the reference program's by a relative error of at most 0.038.
Values may be sent and summed in bfloat16 or wider, within the bound.
A program may use at most 64 MiB of HBM per device.

```python
import math
import jax
import jax.numpy as jnp
import numpy as np
from jax import lax

HD = 128
KVH = 4
GQ = 4
QH = 16
TOK_DEV = 128
GROUP = 3
SEQ_LEN = 65536
DOC_MOST = 1025
DOCS = 127
N_ULY = 4


def draw_queries(key, part):
    key = jax.random.fold_in(key, 11)
    return (2.0 * jax.random.truncated_normal(key, -5.0, 5.0, (SEQ_LEN, QH * HD), jnp.float32)).astype(jnp.bfloat16)


def draw_keys(key, part):
    key = jax.random.fold_in(key, 23)
    return jax.random.truncated_normal(key, -5.0, 5.0, (SEQ_LEN, KVH * HD), jnp.float32).astype(jnp.bfloat16)


def block_levels(key, shape, split, low, high):
    def one(position, blocks):
        heights = jax.random.uniform(jax.random.fold_in(jax.random.fold_in(key, 6), position), (blocks,), jnp.float32, low / len(split), high / len(split))
        return jnp.repeat(jnp.exp(heights), shape[position] // blocks).reshape((-1,) + (1,) * (len(shape) - position - 1))

    gain = one(*split[0])
    for cut in split[1:]:
        gain = gain * one(*cut)
    return gain


def length_profile(number_of, total, most, lean):
    weights = [(1 << 20) // math.isqrt(rank ** lean) + 1 for rank in range(2, number_of + 1)]
    surplus, counts = total - most - (number_of - 1), [1] * (number_of - 1)
    while surplus > 0:
        candidates = [i for i in range(number_of - 1) if counts[i] < most]
        whole, budget = sum([weights[i] for i in candidates]), surplus
        for i in candidates:
            more = min(most - counts[i], max(1, budget * weights[i] // whole), surplus)
            counts[i] = counts[i] + more
            surplus = surplus - more
    return np.array([most] + counts)


def uneven(key, amount, total, most, slope):
    if amount == 2:
        one = jax.random.randint(key, (), max(1, total - most), min(most, total - 1) + 1)
        return jnp.stack([one, total - one])
    sizes = jnp.asarray(length_profile(amount, total, most, slope), jnp.int32)
    pairs = (amount - 1) // 2
    source_of, taker = sizes[1:1 + 2 * pairs:2], sizes[2:2 + 2 * pairs:2]
    room = jnp.minimum(source_of - 1, most - taker)
    moved = jax.random.randint(jax.random.fold_in(key, 1), (pairs,), 0, 1 << 20) % (room + 1)
    sizes = sizes.at[1:1 + 2 * pairs:2].set(source_of - moved).at[2:2 + 2 * pairs:2].set(taker + moved)
    return sizes[jax.random.permutation(jax.random.fold_in(key, 2), amount)]


def noise(own_key, shape, deviation, reach, shards=(), kind=jnp.bfloat16):
    drawn = jax.random.normal(own_key, shape, jnp.float32) * deviation
    if len(shards) > 0:
        drawn = block_levels(own_key, shape, shards, -0.22, 0.18) * drawn
    return jnp.clip(drawn, min=-reach, max=reach).astype(kind)


def setup_inputs(seed: int = 0) -> dict:
    seeds = jax.random.split(jax.random.key(seed), 6)
    return {
        "queries": draw_queries(jax.random.fold_in(seeds[5], 71), 0),
        "keys": draw_keys(jax.random.fold_in(seeds[5], 71), 0),
        "values": noise(seeds[2], (SEQ_LEN, KVH * HD), 1.0, 6.0, ((0, 512),)),
        "out_grad": noise(seeds[3], (SEQ_LEN, QH * HD), 1.0, 6.0, ((0, 512),)),
        "docs": jnp.searchsorted(jnp.cumsum(uneven(seeds[4], DOCS, SEQ_LEN, DOC_MOST, 1)), jnp.arange(SEQ_LEN), side="right").astype(jnp.int32),
    }


def reference(queries, keys, values, out_grad, docs):
    scale = HD ** -0.5
    span = N_ULY * TOK_DEV
    window = GROUP * span
    margin = (GROUP - 1) * span
    count = SEQ_LEN // span
    key_pad = jnp.concatenate([jnp.zeros((margin, KVH * HD), jnp.bfloat16), keys], axis=0)
    value_pad = jnp.concatenate([jnp.zeros((margin, KVH * HD), jnp.bfloat16), values], axis=0)
    doc_pad = jnp.concatenate([jnp.full((margin,), -1, jnp.int32), docs.astype(jnp.int32)], axis=0)

    def one_block(carry, index):
        key_total, value_total = carry
        start = (index * span).astype(jnp.int32)
        query_blk = lax.dynamic_slice_in_dim(queries, start, span, 0).reshape(span, QH, HD)
        grad_blk = lax.dynamic_slice_in_dim(out_grad, start, span, 0).reshape(span, QH, HD)
        query_doc = lax.dynamic_slice_in_dim(docs.astype(jnp.int32), start, span, 0)
        key_all = lax.dynamic_slice_in_dim(key_pad, start, window, 0)
        value_all = lax.dynamic_slice_in_dim(value_pad, start, window, 0)
        key_doc = lax.dynamic_slice_in_dim(doc_pad, start, window, 0)
        query_place = start + jnp.arange(span, dtype=jnp.int32)
        key_place = start - margin + jnp.arange(window, dtype=jnp.int32)
        allowed = (key_place[None, :] <= query_place[:, None]) & (key_doc[None, :] == query_doc[:, None])
        outputs = []
        query_grads = []
        key_parts = []
        value_parts = []
        for group in range(KVH):
            key_win = key_all[:, group * HD:(group + 1) * HD]
            value_win = value_all[:, group * HD:(group + 1) * HD]
            key_part = jnp.zeros((window, HD), jnp.float32)
            value_part = jnp.zeros((window, HD), jnp.float32)
            for inner in range(GQ):
                head = group * GQ + inner
                query_head = query_blk[:, head]
                grad_head = grad_blk[:, head]
                scores = jnp.dot(query_head, key_win.T, preferred_element_type=jnp.float32) * scale
                scores = jnp.where(allowed, scores, -jnp.inf)
                top = jnp.max(scores, axis=1, keepdims=True)
                shifted = jnp.exp(scores - top)
                total = jnp.sum(shifted, axis=1, keepdims=True)
                output = (jnp.dot(shifted.astype(jnp.bfloat16), value_win, preferred_element_type=jnp.float32) / total).astype(jnp.bfloat16)
                lse = top + jnp.log(total)
                probs = jnp.exp(scores - lse)
                value_part = value_part + jnp.dot(probs.astype(jnp.bfloat16).T, grad_head, preferred_element_type=jnp.float32)
                dprob = jnp.dot(grad_head, value_win.T, preferred_element_type=jnp.float32)
                delta = jnp.sum(grad_head.astype(jnp.float32) * output.astype(jnp.float32), axis=1, keepdims=True)
                dscore = (probs * (dprob - delta)).astype(jnp.bfloat16)
                query_grads.append(jnp.dot(dscore, key_win, preferred_element_type=jnp.float32) * scale)
                key_part = key_part + jnp.dot(dscore.T, query_head, preferred_element_type=jnp.float32) * scale
                outputs.append(output)
            key_parts.append(key_part)
            value_parts.append(value_part)
        key_block = jnp.concatenate(key_parts, axis=1)
        value_block = jnp.concatenate(value_parts, axis=1)
        key_total = lax.dynamic_update_slice_in_dim(key_total, lax.dynamic_slice_in_dim(key_total, start, window, 0) + key_block, start, 0)
        value_total = lax.dynamic_update_slice_in_dim(value_total, lax.dynamic_slice_in_dim(value_total, start, window, 0) + value_block, start, 0)
        return (key_total, value_total), (jnp.concatenate(outputs, axis=1), jnp.concatenate(query_grads, axis=1))

    empty = jnp.zeros((SEQ_LEN + margin, KVH * HD), jnp.float32)
    (key_total, value_total), (attended, query_grad) = lax.scan(one_block, (empty, empty), jnp.arange(count, dtype=jnp.int32))
    return (attended.reshape(SEQ_LEN, QH * HD), query_grad.reshape(SEQ_LEN, QH * HD), key_total[margin:], value_total[margin:])
```

```python
import math

import jax
import jax.numpy as jnp
from jax import lax
from jax.experimental import pallas as pl
from jax.experimental.pallas import tpu as pltpu
from jax.sharding import PartitionSpec as P

HD = 128
KVH = 4
QH = 16
PAIRS = 8
TOK = 128
TILES = 9
C2 = HD ** -0.5 * math.log2(math.e)
SCALE = HD ** -0.5
LOW = -1e30
NT = (((1,), (1,)), ((), ()))
F32 = jnp.float32
BF16 = jnp.bfloat16


def kernel(q_hbm, k_hbm, v_hbm, g_hbm, docs_ref, o_hbm, dq_hbm, dk_hbm, dv_hbm,
           kv, dd, qs, gs, gt, s_ref, dp_ref, ot, dqt, m_ref, l_ref, dl_ref,
           ct, rx, o_buf, dq_buf, dk_buf, dv_buf,
           lsem, osem, gsend, grecv, rsend, rrecv):
    x = lax.axis_index("uly")
    blk = lax.axis_index("blk")
    blks = lax.axis_size("blk")
    core = lax.rem(blk, 2)
    xr, x2, xl = lax.rem(x + 1, 4), lax.rem(x + 2, 4), lax.rem(x + 3, 4)
    right, left = {"uly": xr}, {"uly": xl}
    ahead = {"blk": lax.rem(blk + 2, blks)}
    behind = {"blk": lax.rem(blk + blks - 2, blks)}
    sibling = {"blk": blk + 1 - 2 * core}

    loads = [
        pltpu.make_async_copy(k_hbm, kv.at[8 + x, 0], lsem.at[0]),
        pltpu.make_async_copy(v_hbm, kv.at[8 + x, 1], lsem.at[1]),
    ]
    for h in range(QH):
        cols = pl.ds(h * HD, HD)
        loads.append(pltpu.make_async_copy(q_hbm.at[:, cols], qs.at[h], lsem.at[2 + h]))
    for h in range(QH):
        cols = pl.ds(h * HD, HD)
        loads.append(pltpu.make_async_copy(g_hbm.at[:, cols], gs.at[h], lsem.at[2 + QH + h]))
    for load in loads:
        load.start()

    barrier = pltpu.get_barrier_semaphore()
    for dev in (right, left, ahead, behind, sibling):
        pl.semaphore_signal(barrier, inc=1, device_id=dev, device_id_type=pl.DeviceIdType.MESH)
    dd[8 + x] = jnp.broadcast_to(docs_ref[...], (8, TOK))
    loads[0].wait()
    loads[1].wait()
    pl.semaphore_wait(barrier, 5)

    def view(slot, part):
        return dd.at[slot] if part == 2 else kv.at[slot, part]

    def gather_copy(n, src, dst, part, dev):
        return pltpu.make_async_remote_copy(
            src_ref=view(src, part), dst_ref=view(dst, part),
            send_sem=gsend.at[n, part], recv_sem=grecv.at[dst, part],
            device_id=dev, device_id_type=pl.DeviceIdType.MESH)

    def send(n, src, dst, parts, dev):
        for part in parts:
            gather_copy(n, src, dst, part, dev).start()

    def arrived(slot, parts):
        for part in parts:
            gather_copy(0, slot, slot, part, right).wait_recv()

    ALL = (2, 0, 1)
    send(0, 8 + x, 8 + x, (2, 0, 1), right)
    send(1, 8 + x, 8 + x, (2, 1, 0), left)
    send(2, 8 + x, x, ALL, ahead)

    @pl.when(core == 0)
    def _():
        send(3, 8 + x, 4 + x, ALL, sibling)

    for slot in (0, 1, 2, 9, 10, 11):
        ct[slot] = jnp.zeros((2, TOK, KVH * HD), BF16)
    m_ref[...] = jnp.full(m_ref.shape, LOW, F32)
    l_ref[...] = jnp.zeros(l_ref.shape, F32)
    ot[...] = jnp.zeros(ot.shape, F32)
    dqt[...] = jnp.zeros(dqt.shape, F32)
    for load in loads[2:]:
        load.wait()
    for u in range(PAIRS):
        for i in range(2):
            gt[u, :, i * TOK:(i + 1) * TOK] = gs[2 * u + i].astype(F32).T
    docs_row = docs_ref[...]

    def cross(k):
        return x + k + 4 * ((x + k) // 4)

    def pick(order, index):
        slot = order[0]
        for i in range(1, TILES):
            slot = jnp.where(index == i, order[i], slot)
        return slot

    def on_own_neighbours():
        arrived(8 + xl, ALL)
        send(4, 8 + xl, 8 + xl, (2, 0), right)
        arrived(8 + xr, ALL)
        send(5, 8 + xr, 8 + xr, (1,), left)

        @pl.when(core == 0)
        def _():
            send(6, 8 + xl, 4 + xl, ALL, sibling)
            send(7, 8 + xr, 4 + xr, ALL, sibling)

    def on_earlier():
        arrived(x, ALL)
        send(8, x, x, ALL, right)
        send(9, x, x, ALL, left)

        @pl.when(core == 1)
        def _():
            send(3, x, 4 + x, ALL, sibling)

    def on_own_far():
        arrived(8 + x2, ALL)
        send(10, 8 + x2, x2, ALL, ahead)

        @pl.when(core == 0)
        def _():
            send(11, 8 + x2, 4 + x2, ALL, sibling)

    def on_earlier_neighbours():
        for slot in (xl, xr):
            arrived(slot, ALL)

        @pl.when(core == 1)
        def _():
            send(6, xl, 4 + xl, ALL, sibling)
            send(7, xr, 4 + xr, ALL, sibling)

    def on_earlier_far():
        arrived(x2, ALL)

        @pl.when(core == 1)
        def _():
            send(11, x2, 4 + x2, ALL, sibling)

    fwd_order = (8 + x, x, 4 + x, 4 + xr, 4 + xl, cross(1), cross(3), 4 + x2, cross(2))

    def forward(index, carry):
        slot = pick(fwd_order, index)

        @pl.when(index == 1)
        def _():
            on_own_neighbours()
            on_earlier()

        @pl.when(index == 2)
        def _():
            arrived(4 + x, ALL)

        @pl.when(index == 3)
        def _():
            on_own_far()
            on_earlier_neighbours()
            arrived(4 + xr, ALL)
            arrived(4 + xl, ALL)

        @pl.when(index == 7)
        def _():
            on_earlier_far()
            arrived(4 + x2, ALL)

        place = slot - x
        key_docs = jnp.broadcast_to(dd[slot][0:1], (TOK, TOK)).T
        key_at = lax.broadcasted_iota(jnp.int32, (TOK, TOK), 0) + (place - 8) * TOK
        row_at = lax.broadcasted_iota(jnp.int32, (TOK, TOK), 1)
        allowed = (key_docs == docs_row) & (key_at <= row_at)
        bias = jnp.where(allowed, 0.0, LOW).astype(F32)
        bias = jnp.concatenate([bias, bias], axis=1)
        for u in range(PAIRS):
            cols = slice((u // 2) * HD, (u // 2 + 1) * HD)
            key, value = kv[slot, 0, :, cols], kv[slot, 1, :, cols]
            query = qs[2 * u:2 * u + 2].reshape(2 * TOK, HD)
            grad = gs[2 * u:2 * u + 2].reshape(2 * TOK, HD)
            scores = lax.dot_general(key, query, NT, preferred_element_type=F32) * C2 + bias
            s_ref[place, u] = scores
            dp_ref[place, u] = lax.dot_general(value, grad, NT, preferred_element_type=F32)
            top = m_ref[u]
            new_top = jnp.maximum(top, jnp.max(scores, axis=0, keepdims=True))
            factor = jnp.exp2(top - new_top)
            weights = jnp.exp2(scores - new_top)
            m_ref[u] = new_top
            l_ref[u] = l_ref[u] * factor + jnp.sum(weights, axis=0, keepdims=True)
            ot[u] = ot[u] * factor + jnp.dot(
                value.T, weights.astype(BF16), preferred_element_type=F32)
        return carry

    lax.fori_loop(0, TILES, forward, 0)

    for u in range(PAIRS):
        total = l_ref[u]
        out = (ot[u] / total).astype(BF16).astype(F32)
        ot[u] = out
        dl_ref[u] = jnp.sum(out * gt[u], axis=0, keepdims=True)
        m_ref[u] = m_ref[u] + jnp.log2(total)

    def reduce_copy(n, src, dst, part, dev):
        return pltpu.make_async_remote_copy(
            src_ref=ct.at[src, part], dst_ref=rx.at[dst, part],
            send_sem=rsend.at[n, part], recv_sem=rrecv.at[dst, part],
            device_id=dev, device_id_type=pl.DeviceIdType.MESH)

    def give(n, src, dst, parts, dev):
        for part in parts:
            reduce_copy(n, src, dst, part, dev).start()

    def add(slot, dst, parts):
        for part in parts:
            reduce_copy(0, slot, dst, part, right).wait_recv()
            ct[slot, part] = (ct[slot, part].astype(F32) + rx[dst, part].astype(F32)).astype(BF16)

    base = 8 - 8 * core
    BOTH = (0, 1)
    bwd_order = (4 + x2, cross(2), 4 + xr, 4 + xl, cross(1), cross(3), 4 + x, x, 8 + x)

    def backward(index, carry):
        slot = pick(bwd_order, index)
        place = slot - x
        for g in range(KVH):
            cols = slice(g * HD, (g + 1) * HD)
            key = kv[slot, 0, :, cols]
            key_t = key.T
            key_grad = jnp.zeros((TOK, HD), F32)
            value_grad = jnp.zeros((TOK, HD), F32)
            for u in (2 * g, 2 * g + 1):
                query = qs[2 * u:2 * u + 2].reshape(2 * TOK, HD)
                grad = gs[2 * u:2 * u + 2].reshape(2 * TOK, HD)
                probs = jnp.exp2(s_ref[place, u] - m_ref[u])
                dscore = (probs * (dp_ref[place, u] - dl_ref[u])).astype(BF16)
                value_grad += jnp.dot(probs.astype(BF16), grad, preferred_element_type=F32)
                key_grad += jnp.dot(dscore, query, preferred_element_type=F32)
                dqt[u] += jnp.dot(key_t, dscore, preferred_element_type=F32)
            ct[slot, 0, :, cols] = key_grad.astype(BF16)
            ct[slot, 1, :, cols] = value_grad.astype(BF16)

        @pl.when(index == 0)
        def _():
            give(0, 4 + x2, x2, BOTH, sibling)

        @pl.when(index == 1)
        def _():
            add(base + x2, x2, BOTH)
            give(1, x2, 4, BOTH, behind)

        @pl.when(index == 2)
        def _():
            give(2, 4 + xr, xr, BOTH, sibling)

        @pl.when(index == 3)
        def _():
            give(3, 4 + xl, xl, BOTH, sibling)

        @pl.when(index == 5)
        def _():
            add(base + xr, xr, BOTH)
            add(base + xl, xl, BOTH)
            give(4, xr, 8, BOTH, right)
            give(5, xl, 9, BOTH, left)
            give(6, 8 + xr, 6, (1,), right)
            give(7, 8 + xl, 7, (0,), left)

        @pl.when(index == 6)
        def _():
            give(8, 4 + x, x, BOTH, sibling)

        return carry

    lax.fori_loop(0, TILES, backward, 0)

    add(base + x, x, BOTH)
    add(8 + x2, 4, BOTH)
    give(9, 8 + x2, 5, (0,), right)
    give(10, 8 + x2, 5, (1,), left)

    for u in range(PAIRS):
        for i in range(2):
            h = 2 * u + i
            cols, rows = slice(h * HD, (h + 1) * HD), slice(i * TOK, (i + 1) * TOK)
            o_buf[:, cols] = ot[u, :, rows].T.astype(BF16)
            dq_buf[:, cols] = dqt[u, :, rows].T * SCALE
    outs = [
        pltpu.make_async_copy(o_buf, o_hbm, osem.at[0]),
        pltpu.make_async_copy(dq_buf, dq_hbm, osem.at[1]),
        pltpu.make_async_copy(dk_buf, dk_hbm, osem.at[2]),
        pltpu.make_async_copy(dv_buf, dv_hbm, osem.at[3]),
    ]
    outs[0].start()
    outs[1].start()

    add(x, 8, BOTH)
    add(x, 9, BOTH)
    give(11, x, 10, BOTH, behind)
    add(8 + xr, 5, (0,))
    give(6, 8 + xr, 6, (0,), right)
    add(8 + xl, 5, (1,))
    give(7, 8 + xl, 7, (1,), left)

    for part, buf in ((0, dk_buf), (1, dv_buf)):
        total = ct[8 + x, part].astype(F32)
        for dst in (6, 7, 10):
            reduce_copy(0, x, dst, part, right).wait_recv()
            total = total + rx[dst, part].astype(F32)
        buf[...] = total * SCALE if part == 0 else total
        outs[2 + part].start()

    for n in range(12):
        for part in (2, 0, 1):
            if (n, part) in ((4, 1), (5, 0), (5, 2)):
                continue
            gather_copy(n, x, x, part, right).wait_send()
    for n in range(12):
        for part in BOTH:
            if (n, part) in ((9, 1), (10, 0)):
                continue
            reduce_copy(n, x, x, part, right).wait_send()
    for out in outs:
        out.wait()


def on_device(queries, keys, values, out_grad, docs):
    rows, width, kv_width = TOK, QH * HD, KVH * HD
    any_spec = pl.BlockSpec(memory_space=pl.ANY)
    vmem_spec = pl.BlockSpec(memory_space=pltpu.VMEM)
    return pl.pallas_call(
        kernel,
        out_shape=(
            jax.ShapeDtypeStruct((rows, width), BF16),
            jax.ShapeDtypeStruct((rows, width), F32),
            jax.ShapeDtypeStruct((rows, kv_width), F32),
            jax.ShapeDtypeStruct((rows, kv_width), F32),
        ),
        in_specs=[any_spec] * 4 + [vmem_spec],
        out_specs=(any_spec,) * 4,
        scratch_shapes=[
            pltpu.VMEM((12, 2, TOK, kv_width), BF16),
            pltpu.VMEM((12, 8, TOK), jnp.int32),
            pltpu.VMEM((QH, TOK, HD), BF16),
            pltpu.VMEM((QH, TOK, HD), BF16),
            pltpu.VMEM((PAIRS, HD, 2 * TOK), F32),
            pltpu.VMEM((TILES, PAIRS, TOK, 2 * TOK), F32),
            pltpu.VMEM((TILES, PAIRS, TOK, 2 * TOK), F32),
            pltpu.VMEM((PAIRS, HD, 2 * TOK), F32),
            pltpu.VMEM((PAIRS, HD, 2 * TOK), F32),
            pltpu.VMEM((PAIRS, 1, 2 * TOK), F32),
            pltpu.VMEM((PAIRS, 1, 2 * TOK), F32),
            pltpu.VMEM((PAIRS, 1, 2 * TOK), F32),
            pltpu.VMEM((12, 2, TOK, kv_width), BF16),
            pltpu.VMEM((11, 2, TOK, kv_width), BF16),
            pltpu.VMEM((rows, width), BF16),
            pltpu.VMEM((rows, width), F32),
            pltpu.VMEM((rows, kv_width), F32),
            pltpu.VMEM((rows, kv_width), F32),
            pltpu.SemaphoreType.DMA((2 + 2 * QH,)),
            pltpu.SemaphoreType.DMA((4,)),
            pltpu.SemaphoreType.DMA((12, 3)),
            pltpu.SemaphoreType.DMA((12, 3)),
            pltpu.SemaphoreType.DMA((12, 2)),
            pltpu.SemaphoreType.DMA((11, 2)),
        ],
        compiler_params=pltpu.CompilerParams(
            collective_id=0, has_side_effects=True, vmem_limit_bytes=56 * 1024 * 1024),
    )(queries, keys, values, out_grad, docs.reshape(1, TOK))


def solution(mesh):
    spec = P(("blk", "uly"), None)
    return jax.shard_map(
        on_device,
        mesh=mesh,
        in_specs=(spec, spec, spec, spec, P(("blk", "uly"))),
        out_specs=(spec, spec, spec, spec),
        check_vma=False,
    )
```

```python
import math

import jax
import jax.numpy as jnp
from jax import lax
from jax.experimental import pallas as pl
from jax.experimental.pallas import tpu as pltpu
from jax.sharding import PartitionSpec as P

HD = 128
KVH = 4
QH = 16
GQ = 4
TOK = 128
LANES = 4
TILES = 9
C2 = HD ** -0.5 * math.log2(math.e)
SCALE = HD ** -0.5
LOW = -1e30
NT = (((1,), (1,)), ((), ()))
F32 = jnp.float32
BF16 = jnp.bfloat16
MESH = pl.DeviceIdType.MESH
WIDE = GQ * HD


def kernel(q_hbm, k_hbm, v_hbm, g_hbm, docs_ref, o_out, dq_out, dkv_out,
           kv, kt, vt, dd, kd, qs, gs, s_ref, ot, dqt, m_ref, l_ref, dl_ref,
           da, ct, fin, rxs, rxy, o_buf, dq_buf,
           lsem, osem, asend, arecv, bsend, brecv, ssend, srecv, dsem, drecv,
           rssend, rsrecv, rysend, ryrecv, osend, orecv):
    x = lax.axis_index("uly")
    blk = lax.axis_index("blk")
    blks = lax.axis_size("blk")
    core = lax.rem(blk, 2)
    peers = tuple(lax.rem(x + k, 4) for k in (2, 1, 3))
    ahead, behind = {"blk": blk + 2}, {"blk": blk - 2}
    sibling = {"blk": blk + 1 - 2 * core}
    when_ahead, when_behind = pl.when(blk < blks - 2), pl.when(blk >= 2)
    when_before = pl.when(blk >= 1)
    when_core0, when_core1 = pl.when(core == 0), pl.when(core == 1)

    def cols(index, width):
        return pl.ds(pl.multiple_of(index * width, width), width)

    def remote(src, dst, send_sem, recv_sem, dev):
        return pltpu.make_async_remote_copy(
            src_ref=src, dst_ref=dst, send_sem=send_sem, recv_sem=recv_sem,
            device_id=dev, device_id_type=MESH)

    def exchange(part, n):
        peer = peers[n]
        src, dst = (
            (k_hbm.at[:, cols(peer, HD)], kv.at[8 + x, 0]),
            (v_hbm.at[:, cols(peer, HD)], kv.at[8 + x, 1]),
            (dd.at[8 + x], dd.at[8 + x]),
            (q_hbm.at[:, cols(peer, WIDE)], qs.at[x]),
            (g_hbm.at[:, cols(peer, WIDE)], gs.at[x]),
        )[part]
        return remote(src, dst, asend.at[part, n], arecv.at[part, x], {"uly": peer})

    def exchanged(part, n):
        origin = peers[n]
        dst = (kv.at[8 + origin, 0], kv.at[8 + origin, 1], dd.at[8 + origin],
               qs.at[origin], gs.at[origin])[part]
        remote(dst, dst, asend.at[part, n], arecv.at[part, origin], {"uly": origin}).wait_recv()

    loads = [
        pltpu.make_async_copy(k_hbm.at[:, cols(x, HD)], kv.at[8 + x, 0], lsem.at[0]),
        pltpu.make_async_copy(v_hbm.at[:, cols(x, HD)], kv.at[8 + x, 1], lsem.at[1]),
        pltpu.make_async_copy(q_hbm.at[:, cols(x, WIDE)], qs.at[x], lsem.at[2]),
        pltpu.make_async_copy(g_hbm.at[:, cols(x, WIDE)], gs.at[x], lsem.at[3]),
    ]
    for load in loads:
        load.start()

    barrier = pltpu.get_barrier_semaphore()

    def greet(dev):
        pl.semaphore_signal(barrier, inc=1, device_id=dev, device_id_type=MESH)

    for peer in peers:
        greet({"uly": peer})
    greet(sibling)
    when_ahead(lambda: greet(ahead))
    when_behind(lambda: greet(behind))
    dd[8 + x] = jnp.broadcast_to(docs_ref[...], (8, TOK))
    pl.semaphore_wait(barrier, 4 + jnp.where(blk < blks - 2, 1, 0) + jnp.where(blk >= 2, 1, 0))

    for part in (0, 1, 2, 3):
        for n in range(3):
            exchange(part, n).start()

    def forward_block(k):
        return remote(kv.at[8 + k], kv.at[k], bsend.at[k], brecv.at[k], ahead)

    def forward_docs():
        return remote(dd.at[8:12], dd.at[0:4], dsem.at[0], drecv.at[0], ahead)

    def sibling_blocks(row):
        return remote(kv.at[pl.ds(row, 4)], kv.at[4:8], ssend.at[0], srecv.at[0], sibling)

    def sibling_docs(row):
        return remote(dd.at[pl.ds(row, 4)], dd.at[4:8], ssend.at[1], srecv.at[1], sibling)

    loads[0].wait()
    loads[1].wait()
    when_ahead(lambda: forward_block(x).start())

    def absent(row):
        kv[row:row + 4] = jnp.zeros((4, 2, TOK, HD), BF16)
        dd[row:row + 4] = jnp.full((4, 8, TOK), -1, jnp.int32)

    pl.when(blk < 2)(lambda: absent(0))
    pl.when(blk < 1)(lambda: absent(4))

    m_ref[...] = jnp.full(m_ref.shape, LOW, F32)
    l_ref[...] = jnp.zeros(l_ref.shape, F32)
    ot[...] = jnp.zeros(ot.shape, F32)
    dqt[...] = jnp.zeros(dqt.shape, F32)
    da[...] = jnp.zeros(da.shape, F32)

    for n in (1, 2, 0):
        for part in (0, 1, 2):
            exchanged(part, n)
        when_ahead(lambda: forward_block(peers[n]).start())
    when_ahead(lambda: forward_docs().start())

    @when_core0
    def _():
        sibling_blocks(8).start()
        sibling_docs(8).start()

    for n in range(3):
        exchange(4, n).start()

    def prepare(row):
        for t in range(row, row + 4):
            kt[t] = kv[t, 0].T
            vt[t] = kv[t, 1].T
            kd[t] = jnp.broadcast_to(dd[t][0:1], (TOK, TOK)).T

    prepare(8)
    loads[2].wait()
    for n in range(3):
        exchanged(3, n)

    def two_back():
        @when_behind
        def _():
            for k in range(4):
                remote(kv.at[k], kv.at[k], bsend.at[k], brecv.at[k], behind).wait_recv()
            forward_docs().wait_recv()

            @when_core1
            def _():
                sibling_blocks(0).start()
                sibling_docs(0).start()

        prepare(0)

    def one_back():
        @when_before
        def _():
            sibling_blocks(0).wait_recv()
            sibling_docs(0).wait_recv()

        prepare(4)

    def heads(ref, i, p):
        lo = 2 * p * HD
        return jnp.concatenate([ref[i, :, lo:lo + HD], ref[i, :, lo + HD:lo + 2 * HD]], axis=0)

    def tile(one_row, k, i):
        return jnp.where(one_row, 4 + k, jnp.where(i <= k, k, 9 + k))

    def forward(index, carry):
        @pl.when((index == 1) & (core == 0) | (index == 5) & (core == 1))
        def _():
            two_back()

        @pl.when((index == 1) & (core == 1) | (index == 5) & (core == 0))
        def _():
            one_back()

        phase = (index + 3) // 4
        k = index - 1 - 4 * (phase - 1)
        k = jnp.where(index == 0, -1, k)
        one_row = (index > 0) & (lax.rem(phase + core, 2) == 0)
        for i in range(LANES):
            t = tile(one_row, k, i)
            key_at = lax.broadcasted_iota(jnp.int32, (TOK, TOK), 0) + (t - 8 - i) * TOK
            row_at = lax.broadcasted_iota(jnp.int32, (TOK, TOK), 1)
            allowed = (kd[t] == dd[8 + i][0:1]) & (key_at <= row_at)
            bias = jnp.where(allowed, 0.0, LOW).astype(F32)
            bias = jnp.concatenate([bias, bias], axis=1)
            for p in range(2):
                scores = lax.dot_general(
                    kv[t, 0], heads(qs, i, p), NT, preferred_element_type=F32) * C2 + bias
                s_ref[i, t - i, p] = scores
                top = m_ref[i, p]
                new_top = jnp.maximum(top, jnp.max(scores, axis=0, keepdims=True))
                factor = jnp.exp2(top - new_top)
                weights = jnp.exp2(scores - new_top)
                m_ref[i, p] = new_top
                l_ref[i, p] = l_ref[i, p] * factor + jnp.sum(weights, axis=0, keepdims=True)
                ot[i, p] = ot[i, p] * factor + jnp.dot(
                    vt[t], weights.astype(BF16), preferred_element_type=F32)
        return carry

    lax.fori_loop(0, TILES, forward, 0)

    loads[3].wait()
    for n in range(3):
        exchanged(4, n)

    for i in range(LANES):
        for p in range(2):
            total = l_ref[i, p]
            out = (ot[i, p] / total).astype(BF16)
            m_ref[i, p] = m_ref[i, p] + jnp.log2(total)
            for e in range(2):
                lo = (2 * p + e) * HD
                half = out[:, e * TOK:(e + 1) * TOK]
                o_buf[i, :, lo:lo + HD] = half.T
                grad_t = gs[i, :, lo:lo + HD].T.astype(F32)
                dl_ref[i, p, :, e * TOK:(e + 1) * TOK] = jnp.sum(
                    grad_t * half.astype(F32), axis=0, keepdims=True)

    def deliver(kind, n):
        peer = peers[n]
        src, dst = ((o_buf.at[peer], o_out.at[x]), (dq_buf.at[peer], dq_out.at[x]),
                    (fin.at[peer], dkv_out.at[x]))[kind]
        return remote(src, dst, osend.at[kind, n], orecv.at[kind, x], {"uly": peer})

    def delivered(kind, n):
        origin = peers[n]
        dst = (o_out, dq_out, dkv_out)[kind].at[origin]
        remote(dst, dst, osend.at[kind, n], orecv.at[kind, origin], {"uly": origin}).wait_recv()

    keep = [
        pltpu.make_async_copy(o_buf.at[x], o_out.at[x], osem.at[0]),
        pltpu.make_async_copy(dq_buf.at[x], dq_out.at[x], osem.at[1]),
        pltpu.make_async_copy(fin.at[x], dkv_out.at[x], osem.at[2]),
    ]
    keep[0].start()
    for n in range(3):
        deliver(0, n).start()

    def to_sibling(k):
        return remote(ct.at[4 + k], rxs.at[k], rssend.at[k], rsrecv.at[k], sibling)

    def to_behind(k):
        return remote(ct.at[k], rxy.at[k], rysend.at[k], ryrecv.at[k], behind)

    def step(n):
        off = jnp.where(n == 0, 2, jnp.where(n == 1, 1, jnp.where(n == 2, 3, 0)))
        return lax.rem(x + off, 4)

    def backward(index, carry):
        phase = index // 4
        k = jnp.where(index == 8, -1, step(index - 4 * phase))
        one_row = (index < 8) & (lax.rem(phase + core, 2) == 0)
        for i in range(LANES):
            t = tile(one_row, k, i)
            key_grad = jnp.zeros((TOK, HD), F32)
            value_grad = jnp.zeros((TOK, HD), F32)
            for p in range(2):
                query, grad = heads(qs, i, p), heads(gs, i, p)
                probs = jnp.exp2(s_ref[i, t - i, p] - m_ref[i, p])
                dprob = lax.dot_general(kv[t, 1], grad, NT, preferred_element_type=F32)
                dscore = (probs * (dprob - dl_ref[i, p])).astype(BF16)
                value_grad += jnp.dot(probs.astype(BF16), grad, preferred_element_type=F32)
                key_grad += jnp.dot(dscore, query, preferred_element_type=F32)
                dqt[i, p] += jnp.dot(kt[t], dscore, preferred_element_type=F32)
            da[t, 0] += key_grad
            da[t, 1] += value_grad

        @pl.when(one_row)
        def _():
            ct[4 + k] = da[4 + k].astype(BF16)
            when_before(lambda: to_sibling(k).start())

        @pl.when((core == 0) & (phase == 1))
        def _():
            ct[k] = da[k].astype(BF16)
            when_behind(lambda: to_behind(k).start())

        @pl.when((core == 1) & (index >= 2) & (index < 6) & (blk >= 2))
        def _():
            j = step(index - 2)
            to_sibling(j).wait_recv()
            ct[j] = (da[j] + rxs[j].astype(F32)).astype(BF16)
            to_behind(j).start()

        return carry

    lax.fori_loop(0, TILES, backward, 0)

    for i in range(LANES):
        for p in range(2):
            for e in range(2):
                lo = (2 * p + e) * HD
                dq_buf[i, :, lo:lo + HD] = (
                    dqt[i, p, :, e * TOK:(e + 1) * TOK].T * SCALE).astype(BF16)
    keep[1].start()
    for n in range(3):
        deliver(1, n).start()

    @when_core0
    def _():
        for k in range(4):
            to_sibling(k).wait_recv()
            da[8 + k] += rxs[k].astype(F32)

    for n in range(4):
        k = (peers + (x,))[n]

        @when_ahead
        def _():
            to_behind(k).wait_recv()
            da[8 + k] += rxy[k].astype(F32)

        fin[k] = da[8 + k].astype(BF16)
        if n < 3:
            deliver(2, n).start()
    keep[2].start()

    for part in range(5):
        for n in range(3):
            exchange(part, n).wait_send()
    for kind in range(3):
        for n in range(3):
            delivered(kind, n)
            deliver(kind, n).wait_send()
        keep[kind].wait()

    @when_ahead
    def _():
        for k in range(4):
            forward_block(k).wait_send()
        forward_docs().wait_send()

    @pl.when(blk != 1)
    def _():
        sibling_blocks(0).wait_send()
        sibling_docs(0).wait_send()

    @when_before
    def _():
        for k in range(4):
            to_sibling(k).wait_send()

    @when_behind
    def _():
        for k in range(4):
            to_behind(k).wait_send()


def finish(o_ref, dq_ref, dkv_ref, o_out, dq_out, dk_out, dv_out):
    o_out[...] = o_ref[0]
    dq_out[...] = dq_ref[0].astype(F32)
    dk_out[...] = dkv_ref[0, 0].astype(F32) * SCALE
    dv_out[...] = dkv_ref[0, 1].astype(F32)


def on_device(queries, keys, values, out_grad, docs):
    any_spec = pl.BlockSpec(memory_space=pl.ANY)
    vmem_spec = pl.BlockSpec(memory_space=pltpu.VMEM)
    dma = pltpu.SemaphoreType.DMA
    stat = pltpu.VMEM((LANES, 2, 1, 2 * TOK), F32)
    parts = pl.pallas_call(
        kernel,
        out_shape=(
            jax.ShapeDtypeStruct((LANES, TOK, WIDE), BF16),
            jax.ShapeDtypeStruct((LANES, TOK, WIDE), BF16),
            jax.ShapeDtypeStruct((LANES, 2, TOK, HD), BF16),
        ),
        in_specs=[any_spec] * 4 + [vmem_spec],
        out_specs=(any_spec,) * 3,
        scratch_shapes=[
            pltpu.VMEM((12, 2, TOK, HD), BF16),
            pltpu.VMEM((12, HD, TOK), BF16),
            pltpu.VMEM((12, HD, TOK), BF16),
            pltpu.VMEM((12, 8, TOK), jnp.int32),
            pltpu.VMEM((12, TOK, TOK), jnp.int32),
            pltpu.VMEM((LANES, TOK, WIDE), BF16),
            pltpu.VMEM((LANES, TOK, WIDE), BF16),
            pltpu.VMEM((LANES, TILES, 2, TOK, 2 * TOK), F32),
            pltpu.VMEM((LANES, 2, HD, 2 * TOK), F32),
            pltpu.VMEM((LANES, 2, HD, 2 * TOK), F32),
            stat, stat, stat,
            pltpu.VMEM((12, 2, TOK, HD), F32),
            pltpu.VMEM((8, 2, TOK, HD), BF16),
            pltpu.VMEM((4, 2, TOK, HD), BF16),
            pltpu.VMEM((4, 2, TOK, HD), BF16),
            pltpu.VMEM((4, 2, TOK, HD), BF16),
            pltpu.VMEM((LANES, TOK, WIDE), BF16),
            pltpu.VMEM((LANES, TOK, WIDE), BF16),
            dma((4,)), dma((3,)),
            dma((5, 3)), dma((5, 4)),
            dma((4,)), dma((4,)),
            dma((2,)), dma((2,)),
            dma((1,)), dma((1,)),
            dma((4,)), dma((4,)),
            dma((4,)), dma((4,)),
            dma((3, 3)), dma((3, 4)),
        ],
        compiler_params=pltpu.CompilerParams(
            collective_id=0, has_side_effects=True, vmem_limit_bytes=58 * 1024 * 1024),
    )(queries, keys, values, out_grad, docs.reshape(1, TOK))
    wide = pl.BlockSpec((1, TOK, WIDE), lambda i: (i, 0, 0))
    pair = pl.BlockSpec((1, 2, TOK, HD), lambda i: (i, 0, 0, 0))
    wide_out = pl.BlockSpec((TOK, WIDE), lambda i: (0, i))
    head_out = pl.BlockSpec((TOK, HD), lambda i: (0, i))
    return pl.pallas_call(
        finish,
        grid=(LANES,),
        out_shape=(
            jax.ShapeDtypeStruct((TOK, QH * HD), BF16),
            jax.ShapeDtypeStruct((TOK, QH * HD), F32),
            jax.ShapeDtypeStruct((TOK, KVH * HD), F32),
            jax.ShapeDtypeStruct((TOK, KVH * HD), F32),
        ),
        in_specs=[wide, wide, pair],
        out_specs=(wide_out, wide_out, head_out, head_out),
    )(*parts)


def solution(mesh):
    spec = P(("blk", "uly"), None)
    return jax.shard_map(
        on_device,
        mesh=mesh,
        in_specs=(spec, spec, spec, spec, P(("blk", "uly"))),
        out_specs=(spec, spec, spec, spec),
        check_vma=False,
    )
```

```python
import math

import jax
import jax.numpy as jnp
from jax import lax
from jax.experimental import pallas as pl
from jax.experimental.pallas import tpu as pltpu
from jax.sharding import PartitionSpec as P

HD = 128
KVH = 4
QH = 16
GQ = 4
TOK = 128
LANES = 4
TILES = 9
C2 = HD ** -0.5 * math.log2(math.e)
SCALE = HD ** -0.5
LOW = -1e30
F32 = jnp.float32
BF16 = jnp.bfloat16
MESH = pl.DeviceIdType.MESH
WIDE = GQ * HD
FWD_STEP = 1
BWD_STEP = 1


def kernel(q_hbm, k_hbm, v_hbm, g_hbm, docs_ref, o_out, dq_out, dkv_out,
           kv, kt, vt, dd, kd, qs, gs, qt, gt, s_ref, ds_ref, ot, m_ref, l_ref, dl_ref,
           da, ct, fin, rxs, rxy, o_buf, dq_buf,
           lsem, osem, asend, arecv, bsend, brecv, ssend, srecv, dsem, drecv,
           rssend, rsrecv, rysend, ryrecv, osend, orecv):
    x = lax.axis_index("uly")
    blk = lax.axis_index("blk")
    blks = lax.axis_size("blk")
    core = lax.rem(blk, 2)
    peers = tuple(lax.rem(x + k, 4) for k in (2, 1, 3))
    ahead, behind = {"blk": blk + 2}, {"blk": blk - 2}
    sibling = {"blk": blk + 1 - 2 * core}
    when_ahead, when_behind = pl.when(blk < blks - 2), pl.when(blk >= 2)
    when_before = pl.when(blk >= 1)
    when_core0, when_core1 = pl.when(core == 0), pl.when(core == 1)

    def cols(index, width):
        return pl.ds(pl.multiple_of(index * width, width), width)

    def remote(src, dst, send_sem, recv_sem, dev):
        return pltpu.make_async_remote_copy(
            src_ref=src, dst_ref=dst, send_sem=send_sem, recv_sem=recv_sem,
            device_id=dev, device_id_type=MESH)

    def exchange(part, n):
        peer = peers[n]
        src, dst = (
            (k_hbm.at[:, cols(peer, HD)], kv.at[8 + x, 0]),
            (v_hbm.at[:, cols(peer, HD)], kv.at[8 + x, 1]),
            (dd.at[8 + x], dd.at[8 + x]),
            (q_hbm.at[:, cols(peer, WIDE)], qs.at[x]),
            (g_hbm.at[:, cols(peer, WIDE)], gs.at[x]),
        )[part]
        return remote(src, dst, asend.at[part, n], arecv.at[part, x], {"uly": peer})

    def exchanged(part, n):
        origin = peers[n]
        dst = (kv.at[8 + origin, 0], kv.at[8 + origin, 1], dd.at[8 + origin],
               qs.at[origin], gs.at[origin])[part]
        remote(dst, dst, asend.at[part, n], arecv.at[part, origin], {"uly": origin}).wait_recv()

    loads = [
        pltpu.make_async_copy(k_hbm.at[:, cols(x, HD)], kv.at[8 + x, 0], lsem.at[0]),
        pltpu.make_async_copy(v_hbm.at[:, cols(x, HD)], kv.at[8 + x, 1], lsem.at[1]),
        pltpu.make_async_copy(q_hbm.at[:, cols(x, WIDE)], qs.at[x], lsem.at[2]),
        pltpu.make_async_copy(g_hbm.at[:, cols(x, WIDE)], gs.at[x], lsem.at[3]),
    ]
    for load in loads:
        load.start()

    barrier = pltpu.get_barrier_semaphore()

    def greet(dev):
        pl.semaphore_signal(barrier, inc=1, device_id=dev, device_id_type=MESH)

    for peer in peers:
        greet({"uly": peer})
    greet(sibling)
    when_ahead(lambda: greet(ahead))
    when_behind(lambda: greet(behind))
    dd[8 + x] = jnp.broadcast_to(docs_ref[...], (8, TOK))
    pl.semaphore_wait(barrier, 4 + jnp.where(blk < blks - 2, 1, 0) + jnp.where(blk >= 2, 1, 0))

    for part in (0, 1, 2):
        for n in range(3):
            exchange(part, n).start()

    def forward_block(k):
        return remote(kv.at[8 + k], kv.at[k], bsend.at[k], brecv.at[k], ahead)

    def forward_docs():
        return remote(dd.at[8:12], dd.at[0:4], dsem.at[0], drecv.at[0], ahead)

    def sibling_blocks(row):
        return remote(kv.at[pl.ds(row, 4)], kv.at[4:8], ssend.at[0], srecv.at[0], sibling)

    def sibling_docs(row):
        return remote(dd.at[pl.ds(row, 4)], dd.at[4:8], ssend.at[1], srecv.at[1], sibling)

    loads[0].wait()
    loads[1].wait()
    when_ahead(lambda: forward_block(x).start())

    def absent(row):
        kv[row:row + 4] = jnp.zeros((4, 2, TOK, HD), BF16)
        dd[row:row + 4] = jnp.full((4, 8, TOK), -1, jnp.int32)

    pl.when(blk < 2)(lambda: absent(0))
    pl.when(blk < 1)(lambda: absent(4))

    for part in (0, 1):
        for n in range(3):
            exchange(part, n).wait_send()
    for n in range(3):
        exchange(3, n).start()

    m_ref[...] = jnp.full(m_ref.shape, LOW, F32)
    l_ref[...] = jnp.zeros(l_ref.shape, F32)
    ot[...] = jnp.zeros(ot.shape, F32)

    for n in (1, 2, 0):
        for part in (0, 1, 2):
            exchanged(part, n)
        when_ahead(lambda: forward_block(peers[n]).start())
    when_ahead(lambda: forward_docs().start())

    @when_core0
    def _():
        sibling_blocks(8).start()
        sibling_docs(8).start()

    def prepare(row):
        for t in range(row, row + 4):
            kt[t] = kv[t, 0].T
            vt[t] = kv[t, 1].T
            kd[t] = jnp.broadcast_to(dd[t][0:1], (TOK, TOK)).T

    prepare(8)
    for n in range(3):
        exchange(3, n).wait_send()
    for n in range(3):
        exchange(4, n).start()
    loads[2].wait()
    for n in range(3):
        exchanged(3, n)

    def two_back():
        @when_behind
        def _():
            for k in range(4):
                remote(kv.at[k], kv.at[k], bsend.at[k], brecv.at[k], behind).wait_recv()
            forward_docs().wait_recv()

            @when_core1
            def _():
                sibling_blocks(0).start()
                sibling_docs(0).start()

        prepare(0)

    def one_back():
        @when_before
        def _():
            sibling_blocks(0).wait_recv()
            sibling_docs(0).wait_recv()

        prepare(4)

    def heads(ref, i, p):
        lo = 2 * p * HD
        return jnp.concatenate([ref[i, :, lo:lo + HD], ref[i, :, lo + HD:lo + 2 * HD]], axis=0)

    def tile(one_row, k, i):
        return jnp.where(one_row, 4 + k, jnp.where(i <= k, k, 9 + k))

    def stack(parts, axis=0):
        return parts[0] if len(parts) == 1 else jnp.concatenate(parts, axis=axis)

    def forward(one_row, ks):
        for i in range(LANES):
            tiles = [tile(one_row, k, i) for k in ks]
            biases = []
            for t in tiles:
                key_at = lax.broadcasted_iota(jnp.int32, (TOK, TOK), 0) + (t - 8 - i) * TOK
                row_at = lax.broadcasted_iota(jnp.int32, (TOK, TOK), 1)
                allowed = (kd[t] == dd[8 + i][0:1]) & (key_at <= row_at)
                bias = jnp.where(allowed, 0.0, LOW).astype(F32)
                biases.append(jnp.concatenate([bias, bias], axis=1))
            bias = stack(biases)
            keys = stack([kv[t, 0] for t in tiles])
            values_t = stack([vt[t] for t in tiles], 1)
            for p in range(2):
                scores = jnp.dot(keys, qt[i, p], preferred_element_type=F32) * C2 + bias
                for a, t in enumerate(tiles):
                    s_ref[i, t - i, p] = scores[a * TOK:(a + 1) * TOK]
                top = m_ref[i, p]
                new_top = jnp.maximum(top, jnp.max(scores, axis=0, keepdims=True))
                factor = jnp.exp2(top - new_top)
                weights = jnp.exp2(scores - new_top)
                m_ref[i, p] = new_top
                l_ref[i, p] = l_ref[i, p] * factor + jnp.sum(weights, axis=0, keepdims=True)
                ot[i, p] = ot[i, p] * factor + jnp.dot(
                    values_t, weights.astype(BF16), preferred_element_type=F32)

    def forward_some(index, carry):
        turns = 4 // FWD_STEP
        at_start, at_middle = index == 0, index == turns

        @pl.when(at_start & (core == 0) | at_middle & (core == 1))
        def _():
            two_back()

        @pl.when(at_start & (core == 1) | at_middle & (core == 0))
        def _():
            one_back()

        phase = index // turns
        k = FWD_STEP * (index - turns * phase)
        forward(lax.rem(phase + core, 2) == 1, tuple(k + a for a in range(FWD_STEP)))
        return carry

    def turn(ref, out):
        for i in range(LANES):
            for p in range(2):
                out[i, p] = heads(ref, i, p).T

    turn(qs, qt)
    forward(False, (-1,))
    lax.fori_loop(0, 8 // FWD_STEP, forward_some, 0)

    loads[3].wait()
    for n in range(3):
        exchanged(4, n)

    turn(gs, gt)

    for i in range(LANES):
        for p in range(2):
            total = l_ref[i, p]
            out = (ot[i, p] / total).astype(BF16)
            m_ref[i, p] = m_ref[i, p] + jnp.log2(total)
            dl_ref[i, p] = jnp.sum(
                gt[i, p].astype(F32) * out.astype(F32), axis=0, keepdims=True)
            for e in range(2):
                lo = (2 * p + e) * HD
                o_buf[i, :, lo:lo + HD] = out[:, e * TOK:(e + 1) * TOK].T

    def deliver(kind, n):
        peer = peers[n]
        src, dst = ((o_buf.at[peer], o_out.at[x]), (dq_buf.at[peer], dq_out.at[x]),
                    (fin.at[peer], dkv_out.at[x]))[kind]
        return remote(src, dst, osend.at[kind, n], orecv.at[kind, x], {"uly": peer})

    def delivered(kind, n):
        origin = peers[n]
        dst = (o_out, dq_out, dkv_out)[kind].at[origin]
        remote(dst, dst, osend.at[kind, n], orecv.at[kind, origin], {"uly": origin}).wait_recv()

    keep = [
        pltpu.make_async_copy(o_buf.at[x], o_out.at[x], osem.at[0]),
        pltpu.make_async_copy(dq_buf.at[x], dq_out.at[x], osem.at[1]),
        pltpu.make_async_copy(fin.at[x], dkv_out.at[x], osem.at[2]),
    ]
    keep[0].start()
    for n in range(3):
        deliver(0, n).start()

    def to_sibling(k):
        return remote(ct.at[4 + k], rxs.at[k], rssend.at[k], rsrecv.at[k], sibling)

    def to_behind(k):
        return remote(ct.at[k], rxy.at[k], rysend.at[k], ryrecv.at[k], behind)

    def backward(one_row, ks):
        zero = jnp.zeros((TOK, HD), F32)
        early = [[zero, zero] for _ in ks]
        total = [[zero, zero] for _ in ks]
        for i in range(LANES):
            tiles = [tile(one_row, k, i) for k in ks]
            values = stack([kv[t, 1] for t in tiles])
            parts = [0, 0]
            for p in range(2):
                query, grad = heads(qs, i, p), heads(gs, i, p)
                probs = jnp.exp2(stack([s_ref[i, t - i, p] for t in tiles]) - m_ref[i, p])
                dprob = jnp.dot(values, gt[i, p], preferred_element_type=F32)
                dscore = (probs * (dprob - dl_ref[i, p])).astype(BF16)
                parts[0] += jnp.dot(dscore, query, preferred_element_type=F32)
                parts[1] += jnp.dot(probs.astype(BF16), grad, preferred_element_type=F32)
                for a, t in enumerate(tiles):
                    ds_ref[i, p, t - i] = dscore[a * TOK:(a + 1) * TOK]
            for a, k in enumerate(ks):
                for kind in range(2):
                    total[a][kind] += parts[kind][a * TOK:(a + 1) * TOK]
                    early[a][kind] = jnp.where(
                        one_row | (i <= k), total[a][kind], early[a][kind])
        for a, k in enumerate(ks):
            there = jnp.where(one_row, 4 + k, jnp.where(k < 0, 8, k))
            own = jnp.where(one_row, 4, k + 1)
            for kind in range(2):
                ct[there, kind] = early[a][kind].astype(BF16)
                da[own, kind] = total[a][kind] - early[a][kind]

    def backward_some(index, carry):
        turns = 4 // BWD_STEP
        phase = index // turns
        k = BWD_STEP * (index - turns * phase)
        ks = tuple(k + a for a in range(BWD_STEP))
        one_row = lax.rem(phase + core, 2) == 0
        backward(one_row, ks)

        @pl.when(one_row & (blk >= 1))
        def _():
            for j in ks:
                to_sibling(j).start()

        @pl.when((core == 0) & (phase == 1) & (blk >= 2))
        def _():
            for j in ks:
                to_behind(j).start()

        lag = 2 // BWD_STEP

        @pl.when((core == 1) & (index >= lag) & (index < lag + turns) & (blk >= 2))
        def _():
            for a in range(BWD_STEP):
                j = BWD_STEP * (index - lag) + a
                to_sibling(j).wait_recv()
                ct[j] = (ct[j].astype(F32) + rxs[j].astype(F32)).astype(BF16)
                to_behind(j).start()

        return carry

    lax.fori_loop(0, 8 // BWD_STEP, backward_some, 0)
    backward(False, (-1,))

    def query_grads(i):
        keys_t = jnp.concatenate([kt[i + w] for w in range(TILES)], axis=1)
        for p in range(2):
            grad_t = jnp.dot(
                keys_t, ds_ref[i, p].reshape(TILES * TOK, 2 * TOK), preferred_element_type=F32)
            for e in range(2):
                lo = (2 * p + e) * HD
                dq_buf[i, :, lo:lo + HD] = (
                    grad_t[:, e * TOK:(e + 1) * TOK].T * SCALE).astype(BF16)

    for n in range(3):
        query_grads(peers[n])
        deliver(1, n).start()
    query_grads(x)
    keep[1].start()

    @when_core0
    def _():
        for k in range(4):
            to_sibling(k).wait_recv()
            da[k] += rxs[k].astype(F32)

    for n in range(4):
        k = (peers + (x,))[n]

        @when_ahead
        def _():
            to_behind(k).wait_recv()
            da[k] += rxy[k].astype(F32)

        fin[k] = da[k].astype(BF16)
        if n < 3:
            deliver(2, n).start()
    keep[2].start()

    for part in (2, 4):
        for n in range(3):
            exchange(part, n).wait_send()
    for kind in range(3):
        for n in range(3):
            delivered(kind, n)
            deliver(kind, n).wait_send()
        keep[kind].wait()

    @when_ahead
    def _():
        for k in range(4):
            forward_block(k).wait_send()
        forward_docs().wait_send()

    @pl.when(blk != 1)
    def _():
        sibling_blocks(0).wait_send()
        sibling_docs(0).wait_send()

    @when_before
    def _():
        for k in range(4):
            to_sibling(k).wait_send()

    @when_behind
    def _():
        for k in range(4):
            to_behind(k).wait_send()


def finish(o_ref, dq_ref, dkv_ref, o_out, dq_out, dk_out, dv_out,
           o_in, dq_in, dkv_in, dq_f32, dkv_f32, in_sem, out_sem):
    wide = [slice(g * WIDE, (g + 1) * WIDE) for g in range(LANES)]
    dq_loads = [pltpu.make_async_copy(dq_ref.at[g], dq_in.at[g], in_sem.at[g]) for g in range(4)]
    dkv_load = pltpu.make_async_copy(dkv_ref, dkv_in, in_sem.at[4])
    o_loads = [pltpu.make_async_copy(o_ref.at[g], o_in.at[g], in_sem.at[5 + g]) for g in range(4)]
    stores = [pltpu.make_async_copy(dq_f32.at[g], dq_out.at[:, wide[g]], out_sem.at[g])
              for g in range(LANES)]
    stores.append(pltpu.make_async_copy(dkv_f32.at[0], dk_out, out_sem.at[4]))
    stores.append(pltpu.make_async_copy(dkv_f32.at[1], dv_out, out_sem.at[5]))
    stores += [pltpu.make_async_copy(o_in.at[g], o_out.at[:, wide[g]], out_sem.at[6 + g])
               for g in range(LANES)]
    for copy in dq_loads + [dkv_load] + o_loads:
        copy.start()
    for g in range(LANES):
        dq_loads[g].wait()
        dq_f32[g] = dq_in[g].astype(F32)
        stores[g].start()
    dkv_load.wait()
    for g in range(KVH):
        dkv_f32[0, :, g * HD:(g + 1) * HD] = dkv_in[g, 0].astype(F32) * SCALE
        dkv_f32[1, :, g * HD:(g + 1) * HD] = dkv_in[g, 1].astype(F32)
    for copy in stores[4:6]:
        copy.start()
    for g in range(LANES):
        o_loads[g].wait()
        stores[6 + g].start()
    for copy in stores:
        copy.wait()


def on_device(queries, keys, values, out_grad, docs):
    any_spec = pl.BlockSpec(memory_space=pl.ANY)
    vmem_spec = pl.BlockSpec(memory_space=pltpu.VMEM)
    dma = pltpu.SemaphoreType.DMA
    stat = pltpu.VMEM((LANES, 2, 1, 2 * TOK), F32)
    parts = pl.pallas_call(
        kernel,
        out_shape=(
            jax.ShapeDtypeStruct((LANES, TOK, WIDE), BF16),
            jax.ShapeDtypeStruct((LANES, TOK, WIDE), BF16),
            jax.ShapeDtypeStruct((LANES, 2, TOK, HD), BF16),
        ),
        in_specs=[any_spec] * 4 + [vmem_spec],
        out_specs=(any_spec,) * 3,
        scratch_shapes=[
            pltpu.VMEM((12, 2, TOK, HD), BF16),
            pltpu.VMEM((12, HD, TOK), BF16),
            pltpu.VMEM((12, HD, TOK), BF16),
            pltpu.VMEM((12, 8, TOK), jnp.int32),
            pltpu.VMEM((12, TOK, TOK), jnp.int32),
            pltpu.VMEM((LANES, TOK, WIDE), BF16),
            pltpu.VMEM((LANES, TOK, WIDE), BF16),
            pltpu.VMEM((LANES, 2, HD, 2 * TOK), BF16),
            pltpu.VMEM((LANES, 2, HD, 2 * TOK), BF16),
            pltpu.VMEM((LANES, TILES, 2, TOK, 2 * TOK), F32),
            pltpu.VMEM((LANES, 2, TILES, TOK, 2 * TOK), BF16),
            pltpu.VMEM((LANES, 2, HD, 2 * TOK), F32),
            stat, stat, stat,
            pltpu.VMEM((5, 2, TOK, HD), F32),
            pltpu.VMEM((9, 2, TOK, HD), BF16),
            pltpu.VMEM((4, 2, TOK, HD), BF16),
            pltpu.VMEM((4, 2, TOK, HD), BF16),
            pltpu.VMEM((4, 2, TOK, HD), BF16),
            pltpu.VMEM((LANES, TOK, WIDE), BF16),
            pltpu.VMEM((LANES, TOK, WIDE), BF16),
            dma((4,)), dma((3,)),
            dma((5, 3)), dma((5, 4)),
            dma((4,)), dma((4,)),
            dma((2,)), dma((2,)),
            dma((1,)), dma((1,)),
            dma((4,)), dma((4,)),
            dma((4,)), dma((4,)),
            dma((3, 3)), dma((3, 4)),
        ],
        compiler_params=pltpu.CompilerParams(
            collective_id=0, has_side_effects=True, vmem_limit_bytes=58 * 1024 * 1024),
    )(queries, keys, values, out_grad, docs.reshape(1, TOK))
    return pl.pallas_call(
        finish,
        out_shape=(
            jax.ShapeDtypeStruct((TOK, QH * HD), BF16),
            jax.ShapeDtypeStruct((TOK, QH * HD), F32),
            jax.ShapeDtypeStruct((TOK, KVH * HD), F32),
            jax.ShapeDtypeStruct((TOK, KVH * HD), F32),
        ),
        in_specs=[any_spec] * 3,
        out_specs=(any_spec,) * 4,
        scratch_shapes=[
            pltpu.VMEM((LANES, TOK, WIDE), BF16),
            pltpu.VMEM((LANES, TOK, WIDE), BF16),
            pltpu.VMEM((KVH, 2, TOK, HD), BF16),
            pltpu.VMEM((LANES, TOK, WIDE), F32),
            pltpu.VMEM((2, TOK, KVH * HD), F32),
            dma((9,)), dma((10,)),
        ],
    )(*parts)


def solution(mesh):
    spec = P(("blk", "uly"), None)
    return jax.shard_map(
        on_device,
        mesh=mesh,
        in_specs=(spec, spec, spec, spec, P(("blk", "uly"))),
        out_specs=(spec, spec, spec, spec),
        check_vma=False,
    )
```

```python
import math

import jax
import jax.numpy as jnp
from jax import lax
from jax.experimental import pallas as pl
from jax.experimental.pallas import tpu as pltpu
from jax.sharding import PartitionSpec as P

HD = 128
KVH = 4
QH = 16
GQ = 4
TOK = 128
LANES = 4
TILES = 9
C2 = HD ** -0.5 * math.log2(math.e)
SCALE = HD ** -0.5
LOW = -1e30
F32 = jnp.float32
BF16 = jnp.bfloat16
MESH = pl.DeviceIdType.MESH
WIDE = GQ * HD


def kernel(q_hbm, k_hbm, v_hbm, g_hbm, docs_ref, o_out, dq_out, dkv_out,
           kv, kt, vt, dd, kd, qs, gs, qt, gt, s_ref, dp_ref, wb, pb, dsb, ot, m_ref,
           acc, ct, fin, rxs, rxy, o_buf, dq_buf,
           lsem, osem, asend, arecv, bsend, brecv, ssend, srecv, dsem, drecv,
           rssend, rsrecv, rysend, ryrecv, osend, orecv):
    x = lax.axis_index("uly")
    blk = lax.axis_index("blk")
    blks = lax.axis_size("blk")
    core = lax.rem(blk, 2)
    peers = tuple(lax.rem(x + k, 4) for k in (2, 1, 3))
    ahead, behind = {"blk": blk + 2}, {"blk": blk - 2}
    sibling = {"blk": blk + 1 - 2 * core}
    when_ahead, when_behind = pl.when(blk < blks - 2), pl.when(blk >= 2)
    when_before = pl.when(blk >= 1)
    when_core0, when_core1 = pl.when(core == 0), pl.when(core == 1)

    def cols(index, width):
        return pl.ds(pl.multiple_of(index * width, width), width)

    def remote(src, dst, send_sem, recv_sem, dev):
        return pltpu.make_async_remote_copy(
            src_ref=src, dst_ref=dst, send_sem=send_sem, recv_sem=recv_sem,
            device_id=dev, device_id_type=MESH)

    def exchange(part, n):
        peer = peers[n]
        src, dst = (
            (k_hbm.at[:, cols(peer, HD)], kv.at[8 + x, 0]),
            (v_hbm.at[:, cols(peer, HD)], kv.at[8 + x, 1]),
            (dd.at[8 + x], dd.at[8 + x]),
            (q_hbm.at[:, cols(peer, WIDE)], qs.at[x]),
            (g_hbm.at[:, cols(peer, WIDE)], gs.at[x]),
        )[part]
        return remote(src, dst, asend.at[part, n], arecv.at[part, x], {"uly": peer})

    def exchanged(part, n):
        origin = peers[n]
        dst = (kv.at[8 + origin, 0], kv.at[8 + origin, 1], dd.at[8 + origin],
               qs.at[origin], gs.at[origin])[part]
        remote(dst, dst, asend.at[part, n], arecv.at[part, origin], {"uly": origin}).wait_recv()

    loads = [
        pltpu.make_async_copy(k_hbm.at[:, cols(x, HD)], kv.at[8 + x, 0], lsem.at[0]),
        pltpu.make_async_copy(v_hbm.at[:, cols(x, HD)], kv.at[8 + x, 1], lsem.at[1]),
        pltpu.make_async_copy(q_hbm.at[:, cols(x, WIDE)], qs.at[x], lsem.at[2]),
        pltpu.make_async_copy(g_hbm.at[:, cols(x, WIDE)], gs.at[x], lsem.at[3]),
    ]
    for load in loads:
        load.start()

    barrier = pltpu.get_barrier_semaphore()

    def greet(dev):
        pl.semaphore_signal(barrier, inc=1, device_id=dev, device_id_type=MESH)

    for peer in peers:
        greet({"uly": peer})
    greet(sibling)
    for k in range(LANES):
        when_ahead(lambda: greet({"blk": blk + 2, "uly": k}))
        when_behind(lambda: greet({"blk": blk - 2, "uly": k}))
    dd[8 + x] = jnp.broadcast_to(docs_ref[...], (8, TOK))
    pl.semaphore_wait(barrier, 4 + jnp.where(blk < blks - 2, 4, 0) + jnp.where(blk >= 2, 4, 0))

    for part in (0, 1, 2):
        for n in range(3):
            exchange(part, n).start()

    def forward_block(k):
        return remote(kv.at[8 + k], kv.at[k], bsend.at[k], brecv.at[k], ahead)

    def forward_docs():
        return remote(dd.at[8:12], dd.at[0:4], dsem.at[0], drecv.at[0], ahead)

    def sibling_blocks(row):
        return remote(kv.at[pl.ds(row, 4)], kv.at[4:8], ssend.at[0], srecv.at[0], sibling)

    def sibling_docs(row):
        return remote(dd.at[pl.ds(row, 4)], dd.at[4:8], ssend.at[1], srecv.at[1], sibling)

    loads[0].wait()
    loads[1].wait()
    when_ahead(lambda: forward_block(x).start())

    def absent(row):
        kv[row:row + 4] = jnp.zeros((4, 2, TOK, HD), BF16)
        dd[row:row + 4] = jnp.full((4, 8, TOK), -1, jnp.int32)

    pl.when(blk < 2)(lambda: absent(0))
    pl.when(blk < 1)(lambda: absent(4))

    for part in (0, 1):
        for n in range(3):
            exchange(part, n).wait_send()
    for n in range(3):
        exchange(3, n).start()

    acc[...] = jnp.zeros(acc.shape, F32)

    for n in (1, 2, 0):
        for part in (0, 1, 2):
            exchanged(part, n)
        when_ahead(lambda: forward_block(peers[n]).start())
    when_ahead(lambda: forward_docs().start())

    @when_core0
    def _():
        sibling_blocks(8).start()
        sibling_docs(8).start()

    def prepare(row):
        for t in range(row, row + 4):
            vt[t] = kv[t, 1].T
            kd[t] = jnp.broadcast_to(dd[t][0:1], (TOK, TOK)).T

    prepare(8)
    for n in range(3):
        exchange(3, n).wait_send()
    for n in range(3):
        exchange(4, n).start()
    loads[2].wait()
    for n in range(3):
        exchanged(3, n)

    def two_back():
        @when_behind
        def _():
            for k in range(4):
                remote(kv.at[k], kv.at[k], bsend.at[k], brecv.at[k], behind).wait_recv()
            forward_docs().wait_recv()

            @when_core1
            def _():
                sibling_blocks(0).start()
                sibling_docs(0).start()

        prepare(0)

    def one_back():
        @when_before
        def _():
            sibling_blocks(0).wait_recv()
            sibling_docs(0).wait_recv()

        prepare(4)

    def heads(ref, i, p):
        lo = 2 * p * HD
        return jnp.concatenate([ref[i, :, lo:lo + HD], ref[i, :, lo + HD:lo + 2 * HD]], axis=0)

    def turn(ref, out):
        for i in range(LANES):
            for p in range(2):
                out[i, p] = heads(ref, i, p).T

    def step(n):
        off = jnp.where(n == 0, 2, jnp.where(n == 1, 1, jnp.where(n == 2, 3, 0)))
        return lax.rem(x + off, 4)

    def deliver(kind, n, peer):
        src, dst = ((o_buf.at[peer], o_out.at[x]), (dq_buf.at[peer], dq_out.at[x]),
                    (fin.at[peer], dkv_out.at[x]))[kind]
        return remote(src, dst, osend.at[kind, n], orecv.at[kind, x], {"uly": peer})

    def delivered(kind, n):
        origin = peers[n]
        dst = (o_out, dq_out, dkv_out)[kind].at[origin]
        remote(dst, dst, osend.at[kind, n], orecv.at[kind, origin], {"uly": origin}).wait_recv()

    keep = [
        pltpu.make_async_copy(o_buf.at[x], o_out.at[x], osem.at[0]),
        pltpu.make_async_copy(dq_buf.at[x], dq_out.at[x], osem.at[1]),
        pltpu.make_async_copy(fin.at[x], dkv_out.at[x], osem.at[2]),
    ]

    def window(ref, i):
        return jnp.concatenate([ref[i + w] for w in range(TILES)], axis=1)

    def over_rows(part, op):
        return op(part.reshape(TOK // 8, 8, 2 * TOK), axis=0)

    def forward(n, carry):
        i = step(n)
        keys = kv[pl.ds(i, TILES), 0].reshape(TILES * TOK, HD)
        values_t = window(vt, i)
        for p in range(2):
            s_ref[i, p] = jnp.dot(
                keys, qt[i, p], preferred_element_type=F32).reshape(TILES, TOK, 2 * TOK)
        docs_row = dd[8 + i][0:1]
        key_at = lax.broadcasted_iota(jnp.int32, (TOK, TOK), 0)
        row_at = lax.broadcasted_iota(jnp.int32, (TOK, TOK), 1)
        tops, sums = [None, None], [None, None]
        for w in range(TILES):
            allowed = kd[i + w] == docs_row
            if w == TILES - 1:
                allowed = allowed & (key_at <= row_at)
            bias = jnp.where(allowed, 0.0, LOW).astype(F32)
            bias = jnp.concatenate([bias, bias], axis=1)
            for p in range(2):
                scores = s_ref[i, p, w] * C2 + bias
                s_ref[i, p, w] = scores
                part = over_rows(scores, jnp.max)
                tops[p] = part if w == 0 else jnp.maximum(tops[p], part)
        for p in range(2):
            tops[p] = jnp.max(tops[p], axis=0, keepdims=True)
        for w in range(TILES):
            for p in range(2):
                weights = jnp.exp2(s_ref[i, p, w] - tops[p])
                part = over_rows(weights, jnp.sum)
                sums[p] = part if w == 0 else sums[p] + part
                wb[p, w] = weights.astype(BF16)
        for p in range(2):
            total = jnp.sum(sums[p], axis=0, keepdims=True)
            out = jnp.dot(values_t, wb[p].reshape(TILES * TOK, 2 * TOK),
                          preferred_element_type=F32)
            out = (out / total).astype(BF16)
            ot[i, p] = out
            m_ref[i, p] = tops[p] + jnp.log2(total)
            for e in range(2):
                lo = (2 * p + e) * HD
                o_buf[i, :, lo:lo + HD] = out[:, e * TOK:(e + 1) * TOK].T
        pl.when(n < 3)(lambda: deliver(0, n, i).start())
        return carry

    turn(qs, qt)
    two_back()
    one_back()
    lax.fori_loop(0, LANES, forward, 0)
    keep[0].start()
    for t in range(12):
        kt[t] = kv[t, 0].T
    loads[3].wait()

    def backward(n, carry):
        i = lax.rem(x + jnp.where(n == 0, 0, jnp.where(n == 1, 2, jnp.where(n == 2, 1, 3))), 4)
        for m in range(3):
            pl.when(n == m + 1)(lambda: exchanged(4, m))
        for p in range(2):
            gt[i, p] = heads(gs, i, p).T
        values = kv[pl.ds(i, TILES), 1].reshape(TILES * TOK, HD)
        keys_t = window(kt, i)
        deltas = []
        for p in range(2):
            dp_ref[p] = jnp.dot(
                values, gt[i, p], preferred_element_type=F32).reshape(TILES, TOK, 2 * TOK)
            deltas.append(jnp.sum(
                gt[i, p].astype(F32) * ot[i, p].astype(F32), axis=0, keepdims=True))
        for w in range(TILES):
            for p in range(2):
                rows = slice(p * 2 * TOK, (p + 1) * 2 * TOK)
                probs = jnp.exp2(s_ref[i, p, w] - m_ref[i, p])
                pb[w, :, rows] = probs.astype(BF16)
                dsb[w, :, rows] = (probs * (dp_ref[p, w] - deltas[p])).astype(BF16)
        for kind, (left_ref, right_ref) in enumerate(((dsb, qs), (pb, gs))):
            rows = jnp.concatenate([heads(right_ref, i, 0), heads(right_ref, i, 1)], axis=0)
            acc[pl.ds(i, TILES), kind] += jnp.dot(
                left_ref[...].reshape(TILES * TOK, WIDE), rows,
                preferred_element_type=F32).reshape(TILES, TOK, HD)
        for p in range(2):
            grad_t = jnp.dot(
                keys_t, dsb[:, :, p * 2 * TOK:(p + 1) * 2 * TOK].reshape(TILES * TOK, 2 * TOK),
                preferred_element_type=F32)
            for e in range(2):
                lo = (2 * p + e) * HD
                dq_buf[i, :, lo:lo + HD] = (
                    grad_t[:, e * TOK:(e + 1) * TOK].T * SCALE).astype(BF16)
        pl.when(n > 0)(lambda: deliver(1, n - 1, i).start())
        return carry

    def to_sibling(k):
        return remote(ct.at[4 + k], rxs.at[k], rssend.at[k], rsrecv.at[k], sibling)

    def to_behind(k):
        return remote(ct.at[k], dkv_out.at[4 + x], rysend.at[k], ryrecv.at[x],
                      {"blk": blk - 2, "uly": k})

    def from_ahead(k):
        dst = dkv_out.at[4 + k]
        remote(dst, dst, rysend.at[k], ryrecv.at[k], {"blk": blk + 2, "uly": k}).wait_recv()

    lax.fori_loop(0, LANES, backward, 0)
    keep[1].start()

    home = peers + (x,)

    @when_before
    def _():
        for k in home:
            ct[4 + k] = acc[4 + k].astype(BF16)
            to_sibling(k).start()

    @pl.when((core == 0) & (blk >= 2))
    def _():
        for k in home:
            ct[k] = acc[k].astype(BF16)
            to_behind(k).start()

    @pl.when((core == 1) & (blk >= 2))
    def _():
        for k in home:
            to_sibling(k).wait_recv()
            ct[k] = (acc[k] + rxs[k].astype(F32)).astype(BF16)
            to_behind(k).start()

    @when_core0
    def _():
        for k in range(4):
            to_sibling(k).wait_recv()
            acc[8 + k] += rxs[k].astype(F32)

    for n in range(4):
        k = home[n]
        fin[k] = acc[8 + k].astype(BF16)
        if n < 3:
            deliver(2, n, k).start()
    keep[2].start()

    @when_ahead
    def _():
        for k in range(4):
            from_ahead(k)

    @pl.when(blk >= blks - 2)
    def _():
        none_ahead = pltpu.make_async_copy(rxy, dkv_out.at[4:8], osem.at[3])
        rxy[...] = jnp.zeros(rxy.shape, BF16)
        none_ahead.start()
        none_ahead.wait()

    for part in (2, 4):
        for n in range(3):
            exchange(part, n).wait_send()
    for kind in range(3):
        for n in range(3):
            delivered(kind, n)
            deliver(kind, n, peers[n]).wait_send()
        keep[kind].wait()

    @when_ahead
    def _():
        for k in range(4):
            forward_block(k).wait_send()
        forward_docs().wait_send()

    @pl.when(blk != 1)
    def _():
        sibling_blocks(0).wait_send()
        sibling_docs(0).wait_send()

    @when_before
    def _():
        for k in range(4):
            to_sibling(k).wait_send()

    @when_behind
    def _():
        for k in range(4):
            to_behind(k).wait_send()


def finish(o_ref, dq_ref, dkv_ref, o_out, dq_out, dk_out, dv_out,
           o_in, dq_in, dkv_in, dq_f32, dkv_f32, in_sem, out_sem):
    wide = [slice(g * WIDE, (g + 1) * WIDE) for g in range(LANES)]
    dq_loads = [pltpu.make_async_copy(dq_ref.at[g], dq_in.at[g], in_sem.at[g]) for g in range(4)]
    dkv_load = pltpu.make_async_copy(dkv_ref, dkv_in, in_sem.at[4])
    o_loads = [pltpu.make_async_copy(o_ref.at[g], o_in.at[g], in_sem.at[5 + g]) for g in range(4)]
    stores = [pltpu.make_async_copy(dq_f32.at[g], dq_out.at[:, wide[g]], out_sem.at[g])
              for g in range(LANES)]
    stores.append(pltpu.make_async_copy(dkv_f32.at[0], dk_out, out_sem.at[4]))
    stores.append(pltpu.make_async_copy(dkv_f32.at[1], dv_out, out_sem.at[5]))
    stores += [pltpu.make_async_copy(o_in.at[g], o_out.at[:, wide[g]], out_sem.at[6 + g])
               for g in range(LANES)]
    for copy in dq_loads + [dkv_load] + o_loads:
        copy.start()
    for g in range(LANES):
        dq_loads[g].wait()
        dq_f32[g] = dq_in[g].astype(F32)
        stores[g].start()
    dkv_load.wait()
    for g in range(KVH):
        cols = slice(g * HD, (g + 1) * HD)
        key_grad, value_grad = (
            dkv_in[g, kind].astype(F32) + dkv_in[4 + g, kind].astype(F32) for kind in range(2))
        dkv_f32[0, :, cols] = key_grad * SCALE
        dkv_f32[1, :, cols] = value_grad
    for copy in stores[4:6]:
        copy.start()
    for g in range(LANES):
        o_loads[g].wait()
        stores[6 + g].start()
    for copy in stores:
        copy.wait()


def on_device(queries, keys, values, out_grad, docs):
    any_spec = pl.BlockSpec(memory_space=pl.ANY)
    vmem_spec = pl.BlockSpec(memory_space=pltpu.VMEM)
    dma = pltpu.SemaphoreType.DMA
    parts = pl.pallas_call(
        kernel,
        out_shape=(
            jax.ShapeDtypeStruct((LANES, TOK, WIDE), BF16),
            jax.ShapeDtypeStruct((LANES, TOK, WIDE), BF16),
            jax.ShapeDtypeStruct((2 * LANES, 2, TOK, HD), BF16),
        ),
        in_specs=[any_spec] * 4 + [vmem_spec],
        out_specs=(any_spec,) * 3,
        scratch_shapes=[
            pltpu.VMEM((12, 2, TOK, HD), BF16),
            pltpu.VMEM((12, HD, TOK), BF16),
            pltpu.VMEM((12, HD, TOK), BF16),
            pltpu.VMEM((12, 8, TOK), jnp.int32),
            pltpu.VMEM((12, TOK, TOK), jnp.int32),
            pltpu.VMEM((LANES, TOK, WIDE), BF16),
            pltpu.VMEM((LANES, TOK, WIDE), BF16),
            pltpu.VMEM((LANES, 2, HD, 2 * TOK), BF16),
            pltpu.VMEM((LANES, 2, HD, 2 * TOK), BF16),
            pltpu.VMEM((LANES, 2, TILES, TOK, 2 * TOK), F32),
            pltpu.VMEM((2, TILES, TOK, 2 * TOK), F32),
            pltpu.VMEM((2, TILES, TOK, 2 * TOK), BF16),
            pltpu.VMEM((TILES, TOK, WIDE), BF16),
            pltpu.VMEM((TILES, TOK, WIDE), BF16),
            pltpu.VMEM((LANES, 2, HD, 2 * TOK), BF16),
            pltpu.VMEM((LANES, 2, 1, 2 * TOK), F32),
            pltpu.VMEM((12, 2, TOK, HD), F32),
            pltpu.VMEM((8, 2, TOK, HD), BF16),
            pltpu.VMEM((4, 2, TOK, HD), BF16),
            pltpu.VMEM((4, 2, TOK, HD), BF16),
            pltpu.VMEM((4, 2, TOK, HD), BF16),
            pltpu.VMEM((LANES, TOK, WIDE), BF16),
            pltpu.VMEM((LANES, TOK, WIDE), BF16),
            dma((4,)), dma((4,)),
            dma((5, 3)), dma((5, 4)),
            dma((4,)), dma((4,)),
            dma((2,)), dma((2,)),
            dma((1,)), dma((1,)),
            dma((4,)), dma((4,)),
            dma((4,)), dma((4,)),
            dma((3, 3)), dma((3, 4)),
        ],
        compiler_params=pltpu.CompilerParams(
            collective_id=0, has_side_effects=True, vmem_limit_bytes=58 * 1024 * 1024),
    )(queries, keys, values, out_grad, docs.reshape(1, TOK))
    return pl.pallas_call(
        finish,
        out_shape=(
            jax.ShapeDtypeStruct((TOK, QH * HD), BF16),
            jax.ShapeDtypeStruct((TOK, QH * HD), F32),
            jax.ShapeDtypeStruct((TOK, KVH * HD), F32),
            jax.ShapeDtypeStruct((TOK, KVH * HD), F32),
        ),
        in_specs=[any_spec] * 3,
        out_specs=(any_spec,) * 4,
        scratch_shapes=[
            pltpu.VMEM((LANES, TOK, WIDE), BF16),
            pltpu.VMEM((LANES, TOK, WIDE), BF16),
            pltpu.VMEM((2 * KVH, 2, TOK, HD), BF16),
            pltpu.VMEM((LANES, TOK, WIDE), F32),
            pltpu.VMEM((2, TOK, KVH * HD), F32),
            dma((9,)), dma((10,)),
        ],
    )(*parts)


def solution(mesh):
    spec = P(("blk", "uly"), None)
    return jax.shard_map(
        on_device,
        mesh=mesh,
        in_specs=(spec, spec, spec, spec, P(("blk", "uly"))),
        out_specs=(spec, spec, spec, spec),
        check_vma=False,
    )
```

```python
import math

import jax
import jax.numpy as jnp
from jax import lax
from jax.experimental import pallas as pl
from jax.experimental.pallas import tpu as pltpu
from jax.sharding import PartitionSpec as P

HD = 128
KVH = 4
QH = 16
GQ = 4
TOK = 128
LANES = 4
TILES = 9
C2 = HD ** -0.5 * math.log2(math.e)
SCALE = HD ** -0.5
LOW = -1e30
F32 = jnp.float32
BF16 = jnp.bfloat16
MESH = pl.DeviceIdType.MESH
WIDE = GQ * HD


def kernel(q_hbm, k_hbm, v_hbm, g_hbm, docs_ref, o_out, dq_out, dkv_out,
           kv, kt, vt, dd, kd, qs, gs, qt, gt, s_ref, dp_ref, wb, pb, dsb, ot, m_ref,
           acc, ct, fin, rxs, rxy, o_buf, dq_buf,
           lsem, osem, asend, arecv, bsend, brecv, ssend, srecv, dsem, drecv,
           rssend, rsrecv, rysend, ryrecv, osend, orecv):
    x = lax.axis_index("uly")
    blk = lax.axis_index("blk")
    blks = lax.axis_size("blk")
    core = lax.rem(blk, 2)
    peers = tuple(lax.rem(x + k, 4) for k in (2, 1, 3))
    ahead, behind = {"blk": blk + 2}, {"blk": blk - 2}
    sibling = {"blk": blk + 1 - 2 * core}
    when_ahead, when_behind = pl.when(blk < blks - 2), pl.when(blk >= 2)
    when_before = pl.when(blk >= 1)
    when_core0, when_core1 = pl.when(core == 0), pl.when(core == 1)

    def cols(index, width):
        return pl.ds(pl.multiple_of(index * width, width), width)

    def remote(src, dst, send_sem, recv_sem, dev):
        return pltpu.make_async_remote_copy(
            src_ref=src, dst_ref=dst, send_sem=send_sem, recv_sem=recv_sem,
            device_id=dev, device_id_type=MESH)

    def exchange(part, n):
        peer = peers[n]
        src, dst = (
            (k_hbm.at[:, cols(peer, HD)], kv.at[8 + x, 0]),
            (v_hbm.at[:, cols(peer, HD)], kv.at[8 + x, 1]),
            (dd.at[8 + x], dd.at[8 + x]),
            (q_hbm.at[:, cols(peer, WIDE)], qs.at[x]),
            (g_hbm.at[:, cols(peer, WIDE)], gs.at[x]),
        )[part]
        return remote(src, dst, asend.at[part, n], arecv.at[part, x], {"uly": peer})

    def exchanged(part, n):
        origin = peers[n]
        dst = (kv.at[8 + origin, 0], kv.at[8 + origin, 1], dd.at[8 + origin],
               qs.at[origin], gs.at[origin])[part]
        remote(dst, dst, asend.at[part, n], arecv.at[part, origin], {"uly": origin}).wait_recv()

    loads = [
        pltpu.make_async_copy(k_hbm.at[:, cols(x, HD)], kv.at[8 + x, 0], lsem.at[0]),
        pltpu.make_async_copy(v_hbm.at[:, cols(x, HD)], kv.at[8 + x, 1], lsem.at[1]),
        pltpu.make_async_copy(q_hbm.at[:, cols(x, WIDE)], qs.at[x], lsem.at[2]),
        pltpu.make_async_copy(g_hbm.at[:, cols(x, WIDE)], gs.at[x], lsem.at[3]),
    ]
    for load in loads:
        load.start()

    barrier = pltpu.get_barrier_semaphore()

    def greet(dev):
        pl.semaphore_signal(barrier, inc=1, device_id=dev, device_id_type=MESH)

    for peer in peers:
        greet({"uly": peer})
    greet(sibling)
    for k in range(LANES):
        when_ahead(lambda: greet({"blk": blk + 2, "uly": k}))
        when_behind(lambda: greet({"blk": blk - 2, "uly": k}))
    dd[8 + x] = jnp.broadcast_to(docs_ref[...], (8, TOK))
    pl.semaphore_wait(barrier, 4 + jnp.where(blk < blks - 2, 4, 0) + jnp.where(blk >= 2, 4, 0))

    for part in (0, 1, 2):
        for n in range(3):
            exchange(part, n).start()

    def forward_block(k):
        return remote(kv.at[8 + k], kv.at[k], bsend.at[k], brecv.at[k], ahead)

    def forward_docs():
        return remote(dd.at[8:12], dd.at[0:4], dsem.at[0], drecv.at[0], ahead)

    def sibling_blocks(row):
        return remote(kv.at[pl.ds(row, 4)], kv.at[4:8], ssend.at[0], srecv.at[0], sibling)

    def sibling_docs(row):
        return remote(dd.at[pl.ds(row, 4)], dd.at[4:8], ssend.at[1], srecv.at[1], sibling)

    loads[0].wait()
    loads[1].wait()
    when_ahead(lambda: forward_block(x).start())

    def absent(row):
        kv[row:row + 4] = jnp.zeros((4, 2, TOK, HD), BF16)
        dd[row:row + 4] = jnp.full((4, 8, TOK), -1, jnp.int32)

    pl.when(blk < 2)(lambda: absent(0))
    pl.when(blk < 1)(lambda: absent(4))

    for part in (0, 1):
        for n in range(3):
            exchange(part, n).wait_send()
    for n in range(3):
        exchange(3, n).start()

    acc[...] = jnp.zeros(acc.shape, F32)

    for n in (1, 2, 0):
        for part in (0, 1, 2):
            exchanged(part, n)
        when_ahead(lambda: forward_block(peers[n]).start())
    when_ahead(lambda: forward_docs().start())

    @when_core0
    def _():
        sibling_blocks(8).start()
        sibling_docs(8).start()

    def prepare(row):
        for t in range(row, row + 4):
            vt[t] = kv[t, 1].T
            kd[t] = jnp.broadcast_to(dd[t][0:1], (TOK, TOK)).T

    prepare(8)
    for n in range(3):
        exchange(3, n).wait_send()
    for n in range(3):
        exchange(4, n).start()
    loads[2].wait()
    for n in range(3):
        exchanged(3, n)

    def two_back():
        @when_behind
        def _():
            for k in range(4):
                remote(kv.at[k], kv.at[k], bsend.at[k], brecv.at[k], behind).wait_recv()
            forward_docs().wait_recv()

            @when_core1
            def _():
                sibling_blocks(0).start()
                sibling_docs(0).start()

        prepare(0)

    def one_back():
        @when_before
        def _():
            sibling_blocks(0).wait_recv()
            sibling_docs(0).wait_recv()

        prepare(4)

    def heads(ref, i, p):
        lo = 2 * p * HD
        return jnp.concatenate([ref[i, :, lo:lo + HD], ref[i, :, lo + HD:lo + 2 * HD]], axis=0)

    def turn(ref, out):
        for i in range(LANES):
            for p in range(2):
                out[i, p] = heads(ref, i, p).T

    def step(n):
        off = jnp.where(n == 0, 2, jnp.where(n == 1, 1, jnp.where(n == 2, 3, 0)))
        return lax.rem(x + off, 4)

    def deliver(kind, n, peer):
        src, dst = ((o_buf.at[peer], o_out.at[x]), (dq_buf.at[peer], dq_out.at[x]),
                    (fin.at[peer], dkv_out.at[x]))[kind]
        return remote(src, dst, osend.at[kind, n], orecv.at[kind, x], {"uly": peer})

    def delivered(kind, n):
        origin = peers[n]
        dst = (o_out, dq_out, dkv_out)[kind].at[origin]
        remote(dst, dst, osend.at[kind, n], orecv.at[kind, origin], {"uly": origin}).wait_recv()

    keep = [
        pltpu.make_async_copy(o_buf.at[x], o_out.at[x], osem.at[0]),
        pltpu.make_async_copy(dq_buf.at[x], dq_out.at[x], osem.at[1]),
        pltpu.make_async_copy(fin.at[x], dkv_out.at[x], osem.at[2]),
    ]

    def window(ref, i):
        return jnp.concatenate([ref[i + w] for w in range(TILES)], axis=1)

    def over_rows(part, op):
        return op(part.reshape(TOK // 8, 8, 2 * TOK), axis=0)

    def forward(n, carry):
        i = step(n)
        keys = kv[pl.ds(i, TILES), 0].reshape(TILES * TOK, HD)
        values_t = window(vt, i)
        for p in range(2):
            s_ref[i, p] = jnp.dot(
                keys, qt[i, p], preferred_element_type=F32).reshape(TILES, TOK, 2 * TOK)
        docs_row = dd[8 + i][0:1]
        key_at = lax.broadcasted_iota(jnp.int32, (TOK, TOK), 0)
        row_at = lax.broadcasted_iota(jnp.int32, (TOK, TOK), 1)
        tops, sums = [None, None], [None, None]
        for w in range(TILES):
            allowed = kd[i + w] == docs_row
            if w == TILES - 1:
                allowed = allowed & (key_at <= row_at)
            bias = jnp.where(allowed, 0.0, LOW).astype(F32)
            bias = jnp.concatenate([bias, bias], axis=1)
            for p in range(2):
                scores = s_ref[i, p, w] * C2 + bias
                s_ref[i, p, w] = scores
                part = over_rows(scores, jnp.max)
                tops[p] = part if w == 0 else jnp.maximum(tops[p], part)
        for p in range(2):
            tops[p] = jnp.max(tops[p], axis=0, keepdims=True)
        for w in range(TILES):
            for p in range(2):
                weights = jnp.exp2(s_ref[i, p, w] - tops[p])
                part = over_rows(weights, jnp.sum)
                sums[p] = part if w == 0 else sums[p] + part
                wb[p, w] = weights.astype(BF16)
        for p in range(2):
            total = jnp.sum(sums[p], axis=0, keepdims=True)
            out = jnp.dot(values_t, wb[p].reshape(TILES * TOK, 2 * TOK),
                          preferred_element_type=F32)
            out = (out / total).astype(BF16)
            ot[i, p] = out
            m_ref[i, p] = tops[p] + jnp.log2(total)
            for e in range(2):
                lo = (2 * p + e) * HD
                o_buf[i, :, lo:lo + HD] = out[:, e * TOK:(e + 1) * TOK].T
        pl.when(n < 3)(lambda: deliver(0, n, i).start())
        return carry

    turn(qs, qt)
    two_back()
    one_back()
    lax.fori_loop(0, LANES, forward, 0)
    keep[0].start()
    for t in range(12):
        kt[t] = kv[t, 0].T
    loads[3].wait()

    def backward(n, carry):
        i = lax.rem(x + jnp.where(n == 0, 0, jnp.where(n == 1, 2, jnp.where(n == 2, 1, 3))), 4)
        for m in range(3):
            pl.when(n == m + 1)(lambda: exchanged(4, m))
        for p in range(2):
            gt[i, p] = heads(gs, i, p).T
        values = kv[pl.ds(i, TILES), 1].reshape(TILES * TOK, HD)
        keys_t = window(kt, i)
        deltas = []
        for p in range(2):
            dp_ref[p] = jnp.dot(
                values, gt[i, p], preferred_element_type=F32).reshape(TILES, TOK, 2 * TOK)
            deltas.append(jnp.sum(
                gt[i, p].astype(F32) * ot[i, p].astype(F32), axis=0, keepdims=True))
        for w in range(TILES):
            for p in range(2):
                rows = slice(p * 2 * TOK, (p + 1) * 2 * TOK)
                probs = jnp.exp2(s_ref[i, p, w] - m_ref[i, p])
                pb[w, :, rows] = probs.astype(BF16)
                dsb[w, :, rows] = (probs * (dp_ref[p, w] - deltas[p])).astype(BF16)
        for kind, (left_ref, right_ref) in enumerate(((dsb, qs), (pb, gs))):
            rows = jnp.concatenate([heads(right_ref, i, 0), heads(right_ref, i, 1)], axis=0)
            acc[pl.ds(i, TILES), kind] += jnp.dot(
                left_ref[...].reshape(TILES * TOK, WIDE), rows,
                preferred_element_type=F32).reshape(TILES, TOK, HD)
        for p in range(2):
            grad_t = jnp.dot(
                keys_t, dsb[:, :, p * 2 * TOK:(p + 1) * 2 * TOK].reshape(TILES * TOK, 2 * TOK),
                preferred_element_type=F32)
            for e in range(2):
                lo = (2 * p + e) * HD
                dq_buf[i, :, lo:lo + HD] = (
                    grad_t[:, e * TOK:(e + 1) * TOK].T * SCALE).astype(BF16)
        pl.when(n > 0)(lambda: deliver(1, n - 1, i).start())
        return carry

    def to_sibling(k):
        return remote(ct.at[4 + k], rxs.at[k], rssend.at[k], rsrecv.at[k], sibling)

    def to_behind(k):
        return remote(ct.at[k], dkv_out.at[4 + x], rysend.at[k], ryrecv.at[x],
                      {"blk": blk - 2, "uly": k})

    def from_ahead(k):
        dst = dkv_out.at[4 + k]
        remote(dst, dst, rysend.at[k], ryrecv.at[k], {"blk": blk + 2, "uly": k}).wait_recv()

    lax.fori_loop(0, LANES, backward, 0)
    keep[1].start()

    home = peers + (x,)

    @when_before
    def _():
        for k in home:
            ct[4 + k] = acc[4 + k].astype(BF16)
            to_sibling(k).start()

    @pl.when((core == 0) & (blk >= 2))
    def _():
        for k in home:
            ct[k] = acc[k].astype(BF16)
            to_behind(k).start()

    def own_grads():
        for n in range(4):
            k = home[n]
            fin[k] = acc[8 + k].astype(BF16)
            if n < 3:
                deliver(2, n, k).start()

    when_core1(own_grads)

    @pl.when((core == 1) & (blk >= 2))
    def _():
        for k in home:
            to_sibling(k).wait_recv()
            ct[k] = (acc[k] + rxs[k].astype(F32)).astype(BF16)
            to_behind(k).start()

    @when_core0
    def _():
        for k in range(4):
            to_sibling(k).wait_recv()
            acc[8 + k] += rxs[k].astype(F32)
        own_grads()

    keep[2].start()

    @when_ahead
    def _():
        for k in range(4):
            from_ahead(k)

    @pl.when(blk >= blks - 2)
    def _():
        none_ahead = pltpu.make_async_copy(rxy, dkv_out.at[4:8], osem.at[3])
        rxy[...] = jnp.zeros(rxy.shape, BF16)
        none_ahead.start()
        none_ahead.wait()

    for part in (2, 4):
        for n in range(3):
            exchange(part, n).wait_send()
    for kind in range(3):
        for n in range(3):
            delivered(kind, n)
            deliver(kind, n, peers[n]).wait_send()
        keep[kind].wait()

    @when_ahead
    def _():
        for k in range(4):
            forward_block(k).wait_send()
        forward_docs().wait_send()

    @pl.when(blk != 1)
    def _():
        sibling_blocks(0).wait_send()
        sibling_docs(0).wait_send()

    @when_before
    def _():
        for k in range(4):
            to_sibling(k).wait_send()

    @when_behind
    def _():
        for k in range(4):
            to_behind(k).wait_send()


def finish(o_ref, dq_ref, dkv_ref, o_out, dq_out, dk_out, dv_out,
           o_in, dq_in, dkv_in, dq_f32, dkv_f32, in_sem, out_sem):
    wide = [slice(g * WIDE, (g + 1) * WIDE) for g in range(LANES)]
    dq_loads = [pltpu.make_async_copy(dq_ref.at[g], dq_in.at[g], in_sem.at[g]) for g in range(4)]
    dkv_load = pltpu.make_async_copy(dkv_ref, dkv_in, in_sem.at[4])
    o_loads = [pltpu.make_async_copy(o_ref.at[g], o_in.at[g], in_sem.at[5 + g]) for g in range(4)]
    stores = [pltpu.make_async_copy(dq_f32.at[g], dq_out.at[:, wide[g]], out_sem.at[g])
              for g in range(LANES)]
    stores.append(pltpu.make_async_copy(dkv_f32.at[0], dk_out, out_sem.at[4]))
    stores.append(pltpu.make_async_copy(dkv_f32.at[1], dv_out, out_sem.at[5]))
    stores += [pltpu.make_async_copy(o_in.at[g], o_out.at[:, wide[g]], out_sem.at[6 + g])
               for g in range(LANES)]
    for copy in dq_loads + [dkv_load] + o_loads:
        copy.start()
    for g in range(LANES):
        dq_loads[g].wait()
        dq_f32[g] = dq_in[g].astype(F32)
        stores[g].start()
    dkv_load.wait()
    for g in range(KVH):
        cols = slice(g * HD, (g + 1) * HD)
        key_grad, value_grad = (
            dkv_in[g, kind].astype(F32) + dkv_in[4 + g, kind].astype(F32) for kind in range(2))
        dkv_f32[0, :, cols] = key_grad * SCALE
        dkv_f32[1, :, cols] = value_grad
    for copy in stores[4:6]:
        copy.start()
    for g in range(LANES):
        o_loads[g].wait()
        stores[6 + g].start()
    for copy in stores:
        copy.wait()


def on_device(queries, keys, values, out_grad, docs):
    any_spec = pl.BlockSpec(memory_space=pl.ANY)
    vmem_spec = pl.BlockSpec(memory_space=pltpu.VMEM)
    dma = pltpu.SemaphoreType.DMA
    parts = pl.pallas_call(
        kernel,
        out_shape=(
            jax.ShapeDtypeStruct((LANES, TOK, WIDE), BF16),
            jax.ShapeDtypeStruct((LANES, TOK, WIDE), BF16),
            jax.ShapeDtypeStruct((2 * LANES, 2, TOK, HD), BF16),
        ),
        in_specs=[any_spec] * 4 + [vmem_spec],
        out_specs=(any_spec,) * 3,
        scratch_shapes=[
            pltpu.VMEM((12, 2, TOK, HD), BF16),
            pltpu.VMEM((12, HD, TOK), BF16),
            pltpu.VMEM((12, HD, TOK), BF16),
            pltpu.VMEM((12, 8, TOK), jnp.int32),
            pltpu.VMEM((12, TOK, TOK), jnp.int32),
            pltpu.VMEM((LANES, TOK, WIDE), BF16),
            pltpu.VMEM((LANES, TOK, WIDE), BF16),
            pltpu.VMEM((LANES, 2, HD, 2 * TOK), BF16),
            pltpu.VMEM((LANES, 2, HD, 2 * TOK), BF16),
            pltpu.VMEM((LANES, 2, TILES, TOK, 2 * TOK), F32),
            pltpu.VMEM((2, TILES, TOK, 2 * TOK), F32),
            pltpu.VMEM((2, TILES, TOK, 2 * TOK), BF16),
            pltpu.VMEM((TILES, TOK, WIDE), BF16),
            pltpu.VMEM((TILES, TOK, WIDE), BF16),
            pltpu.VMEM((LANES, 2, HD, 2 * TOK), BF16),
            pltpu.VMEM((LANES, 2, 1, 2 * TOK), F32),
            pltpu.VMEM((12, 2, TOK, HD), F32),
            pltpu.VMEM((8, 2, TOK, HD), BF16),
            pltpu.VMEM((4, 2, TOK, HD), BF16),
            pltpu.VMEM((4, 2, TOK, HD), BF16),
            pltpu.VMEM((4, 2, TOK, HD), BF16),
            pltpu.VMEM((LANES, TOK, WIDE), BF16),
            pltpu.VMEM((LANES, TOK, WIDE), BF16),
            dma((4,)), dma((4,)),
            dma((5, 3)), dma((5, 4)),
            dma((4,)), dma((4,)),
            dma((2,)), dma((2,)),
            dma((1,)), dma((1,)),
            dma((4,)), dma((4,)),
            dma((4,)), dma((4,)),
            dma((3, 3)), dma((3, 4)),
        ],
        compiler_params=pltpu.CompilerParams(
            collective_id=0, has_side_effects=True, vmem_limit_bytes=58 * 1024 * 1024),
    )(queries, keys, values, out_grad, docs.reshape(1, TOK))
    return pl.pallas_call(
        finish,
        out_shape=(
            jax.ShapeDtypeStruct((TOK, QH * HD), BF16),
            jax.ShapeDtypeStruct((TOK, QH * HD), F32),
            jax.ShapeDtypeStruct((TOK, KVH * HD), F32),
            jax.ShapeDtypeStruct((TOK, KVH * HD), F32),
        ),
        in_specs=[any_spec] * 3,
        out_specs=(any_spec,) * 4,
        scratch_shapes=[
            pltpu.VMEM((LANES, TOK, WIDE), BF16),
            pltpu.VMEM((LANES, TOK, WIDE), BF16),
            pltpu.VMEM((2 * KVH, 2, TOK, HD), BF16),
            pltpu.VMEM((LANES, TOK, WIDE), F32),
            pltpu.VMEM((2, TOK, KVH * HD), F32),
            dma((9,)), dma((10,)),
        ],
    )(*parts)


def solution(mesh):
    spec = P(("blk", "uly"), None)
    return jax.shard_map(
        on_device,
        mesh=mesh,
        in_specs=(spec, spec, spec, spec, P(("blk", "uly"))),
        out_specs=(spec, spec, spec, spec),
        check_vma=False,
    )
```
